32 devices in a mesh: gx: 2 (over x), gy: 4 (over y, core), gz: 4 (over z).
Axes of the slice: x: 2, y: 2, z: 4, core: 2. Of those that a mesh axis runs over, the one named last changes fastest.
Arguments:
- tokens: bfloat16 [8192, 768], P(('gx', 'gy', 'gz')), may hold values from -6 to 6
- norm_gain: float32 [768], replicated, may hold values from 0.5 to 1.5
- w_qkv: bfloat16 [768, 2304], replicated
- w_out: bfloat16 [768, 768], replicated, may hold values from -0.21875 to 0.21875
- send_rows: int32 [32, 7, 32], P(('gx', 'gy', 'gz')), may hold values from -1 to 255, as said below
- window_rows: int32 [32, 512], P(('gx', 'gy', 'gz')), may hold values from -1 to 479, as said below
- grad_out: bfloat16 [8192, 768], P(('gx', 'gy', 'gz')), may hold values from -6 to 6
Outputs:
- block_out: bfloat16 [8192, 768], P(('gx', 'gy', 'gz'))
- grad_tokens: bfloat16 [8192, 768], P(('gx', 'gy', 'gz'))
- grad_gain: float32 [768], P(('gx', 'gy', 'gz'))
- grad_w_qkv: float32 [768, 2304], P(('gx', 'gy', 'gz'))
- grad_w_out: float32 [768, 768], P(('gx', 'gy', 'gz'))
The draws below stay inside these ranges and needn't reach their ends.
Inputs may be any that keep to these rules, and one draw needn't show every extreme that they name: `send_rows`: entries are rows of the tile (0 to 255) or -1 for empty; in each list the rows come first; a row stands in at most one list of its tile; a tile at the upper end of an axis has no rows in lists toward that axis; tile 0 fills all 7 lists. `window_rows`: entries index the owner's row list (256 own rows, then the 7 received lists of 32 in order k) or are -1 for padding; every own row that no list sends away and every non-empty received entry fills exactly one slot, nothing else does; a device's filled slots make whole windows but one.
All inputs are finite; a program needn't handle non-finite values.
Results may differ from the reference program's by a relative error of at most 0.018.
Values may be sent and summed in bfloat16 or wider, within the bound.
A program may use at most 128 MiB of HBM per device.

```python
import math
import jax
import jax.numpy as jnp
from jax import lax

D = 768
HEADS = 12
HDIM = 64
TOK_DEV = 256
WCAP = 128
WIN_DEV = 4
SLOTS = 512
TOKENS = 8192
N_GX = 2
N_GY = 4
N_GZ = 4


def layout(key):
    devices = N_GX * N_GY * N_GZ
    bcap = TOK_DEV // 8
    span = TOK_DEV + 7 * bcap
    slots = WIN_DEV * WCAP
    key_order, key_count, key_fill, key_window = jax.random.split(key, 4)
    orders = jax.vmap(lambda k: jax.random.permutation(k, TOK_DEV))(jax.random.split(key_order, devices)).astype(jnp.int32)
    orders = (orders + (TOK_DEV - 1) - orders[:, :1]) % TOK_DEV
    counts = jax.random.randint(key_count, (devices, 7), max(bcap // 2, 1), bcap + 1).astype(jnp.int32)
    device = jnp.arange(devices, dtype=jnp.int32)
    coord_x = device // (N_GY * N_GZ)
    coord_y = device // N_GZ % N_GY
    coord_z = device % N_GZ
    direction = jnp.arange(1, 8, dtype=jnp.int32)
    step_x = direction // 4
    step_y = direction // 2 % 2
    step_z = direction % 2
    leaves = (coord_x[:, None] + step_x[None, :] >= N_GX) | (coord_y[:, None] + step_y[None, :] >= N_GY) | (coord_z[:, None] + step_z[None, :] >= N_GZ)
    counts = jnp.where(leaves, 0, counts)
    counts = counts.at[0].set(bcap)
    position = jnp.arange(bcap, dtype=jnp.int32)
    base = (direction[:, None] - 1) * bcap + position[None, :]
    chosen = orders[:, base]
    send = jnp.where(position[None, None, :] < counts[:, :, None], chosen, -1).astype(jnp.int32)
    ranks = jax.vmap(lambda o: jnp.zeros(TOK_DEV, jnp.int32).at[o].set(jnp.arange(TOK_DEV, dtype=jnp.int32)))(orders)
    block = jnp.minimum(ranks // bcap, 6)
    limit = jnp.take_along_axis(counts, block, axis=1)
    kept = (ranks >= 7 * bcap) | (ranks % bcap >= limit)
    src_x = coord_x[:, None] - step_x[None, :]
    src_y = coord_y[:, None] - step_y[None, :]
    src_z = coord_z[:, None] - step_z[None, :]
    inside = (src_x >= 0) & (src_y >= 0) & (src_z >= 0)
    source = jnp.where(inside, (src_x * N_GY + src_y) * N_GZ + src_z, 0).astype(jnp.int32)
    entries = send[source, direction[None, :] - 1]
    arrived = inside[:, :, None] & (entries >= 0)
    valid = jnp.concatenate([kept, arrived.reshape(devices, 7 * bcap)], axis=1)
    scores = jax.vmap(lambda k: jax.random.permutation(k, span))(jax.random.split(key_fill, devices)).astype(jnp.int32)
    scores = jnp.where(valid, scores, scores + span)
    ordered = jnp.argsort(scores, axis=1, stable=True).astype(jnp.int32)
    filled = jnp.sum(valid.astype(jnp.int32), axis=1)
    place = jnp.arange(slots, dtype=jnp.int32)
    sequence = jnp.where(place[None, :] < filled[:, None], ordered[:, jnp.minimum(place, span - 1)], -1)
    key_outer, key_inner = jax.random.split(key_window, 2)
    window_order = jax.vmap(lambda k: jax.random.permutation(k, WIN_DEV))(jax.random.split(key_outer, devices)).astype(jnp.int32)
    inner_order = jax.vmap(lambda k: jax.random.permutation(k, WCAP))(jax.random.split(key_inner, devices * WIN_DEV)).astype(jnp.int32)
    inner_order = inner_order.reshape(devices, WIN_DEV, WCAP)
    index = (window_order[:, :, None] * WCAP + inner_order).reshape(devices, slots)
    table = jnp.take_along_axis(sequence, index, axis=1).astype(jnp.int32)
    return (send, table)


def draw_send_rows(key, part):
    shared = layout(key)
    return shared[0]


def draw_window_rows(key, part):
    shared = layout(key)
    return shared[1]


def draw_w_qkv(key, part):
    key = jax.random.fold_in(key, 3)
    base = jnp.clip(jax.random.normal(key, (D, 3 * D), jnp.float32), -4.0, 4.0) / math.sqrt(D)
    return base.astype(jnp.bfloat16)


def levels(key, extent, pieces, least, high):
    gain = 1.0
    for dim, blocks in pieces:
        steps = jax.random.uniform(jax.random.fold_in(jax.random.fold_in(key, 6), dim), (blocks,), jnp.float32, least / len(pieces), high / len(pieces))
        gain = gain * jnp.repeat(jnp.exp(steps), extent[dim] // blocks).reshape((-1,) + (1,) * (len(extent) - 1 - dim))
    return gain


def bell_draw(own_key, shape, scale, most, shards=(), held_as=jnp.bfloat16):
    level = levels(own_key, shape, shards, -0.22, 0.18) if shards else 1.0
    drawn = jax.random.normal(own_key, shape, jnp.float32) * scale * level
    return jnp.minimum(jnp.maximum(drawn, -most), most).astype(held_as)


def setup_inputs(seed: int = 0) -> dict:
    splits = jax.random.split(jax.random.key(seed), 8)
    tokens = bell_draw(splits[0], (TOKENS, D), 1.0, 6.0, ((0, 32),))
    norm_gain = jnp.clip(1.0 + 0.1 * jax.random.normal(splits[1], (D,), jnp.float32), 0.5, 1.5)
    w_qkv = draw_w_qkv(jax.random.fold_in(splits[7], 71), 0)
    w_out = bell_draw(splits[3], (D, D), D ** -0.5, 0.21875)
    send_rows = draw_send_rows(jax.random.fold_in(splits[7], 71), 0)
    window_rows = draw_window_rows(jax.random.fold_in(splits[7], 71), 0)
    grad_out = bell_draw(splits[6], (TOKENS, D), 1.0, 6.0, ((0, 32),))
    return {"tokens": tokens, "norm_gain": norm_gain, "w_qkv": w_qkv, "w_out": w_out, "send_rows": send_rows, "window_rows": window_rows, "grad_out": grad_out}


epsilon = 1e-06
big_negative = -1e+30

def take_rows(table, index):
    safe = jnp.maximum(index, 0).astype(jnp.int32)
    taken = jnp.take(table, safe, axis=0)
    return jnp.where((index >= 0)[..., None], taken, jnp.zeros((), table.dtype))

def spread_rows(values, index, length):
    target = jnp.where(index >= 0, index, length).astype(jnp.int32)
    empty = jnp.zeros((length, values.shape[-1]), values.dtype)
    return empty.at[target].set(values, mode='drop')

def slot_tokens(send_rows, window_rows):
    devices = N_GX * N_GY * N_GZ
    device = jnp.arange(devices, dtype=jnp.int32)
    coord_x = device // (N_GY * N_GZ)
    coord_y = device // N_GZ % N_GY
    coord_z = device % N_GZ
    columns = [device[:, None] * TOK_DEV + jnp.arange(TOK_DEV, dtype=jnp.int32)[None, :]]
    for direction in range(1, 8):
        src_x = coord_x - direction // 4
        src_y = coord_y - direction // 2 % 2
        src_z = coord_z - direction % 2
        inside = (src_x >= 0) & (src_y >= 0) & (src_z >= 0)
        source = jnp.where(inside, (src_x * N_GY + src_y) * N_GZ + src_z, 0).astype(jnp.int32)
        entries = send_rows[source, direction - 1]
        usable = inside[:, None] & (entries >= 0)
        columns.append(jnp.where(usable, source[:, None] * TOK_DEV + entries, -1).astype(jnp.int32))
    table = jnp.concatenate(columns, axis=1)
    picked = jnp.take_along_axis(table, jnp.maximum(window_rows, 0).astype(jnp.int32), axis=1)
    return jnp.where(window_rows >= 0, picked, -1).astype(jnp.int32)

def split_heads(packed):
    split = packed.reshape(WIN_DEV, WCAP, 3, HEADS, HDIM).astype(jnp.float32)
    return (split[:, :, 0], split[:, :, 1], split[:, :, 2])

def attend(packed, valid):
    query, keys, values = split_heads(packed)
    scores = jnp.einsum('wqhd,wkhd->whqk', query, keys) * HDIM ** (-0.5)
    scores = jnp.where(valid[:, None, None, :], scores, big_negative)
    top = lax.optimization_barrier(jnp.max(scores, axis=-1, keepdims=True))
    expo = jnp.exp(scores - top)
    probs = expo / lax.optimization_barrier(jnp.sum(expo, axis=-1, keepdims=True))
    weights = lax.optimization_barrier(probs.astype(jnp.bfloat16))
    mixed = jnp.einsum('whqk,wkhd->wqhd', weights.astype(jnp.float32), values).astype(jnp.bfloat16)
    return (mixed.reshape(SLOTS, D), probs, weights)

def attend_back(packed, probs, weights, delta_slots):
    query, keys, values = split_heads(packed)
    grad_delta = delta_slots.reshape(WIN_DEV, WCAP, HEADS, HDIM).astype(jnp.float32)
    dweights = jnp.einsum('wqhd,wkhd->whqk', grad_delta, values)
    dscores = probs * (dweights - lax.optimization_barrier(jnp.sum(dweights * probs, axis=-1, keepdims=True)))
    dscaled = lax.optimization_barrier((dscores * HDIM ** (-0.5)).astype(jnp.bfloat16)).astype(jnp.float32)
    dquery = jnp.einsum('whqk,wkhd->wqhd', dscaled, keys)
    dkeys = jnp.einsum('whqk,wqhd->wkhd', dscaled, query)
    dvalues = jnp.einsum('whqk,wqhd->wkhd', weights.astype(jnp.float32), grad_delta)
    joined = jnp.stack([dquery, dkeys, dvalues], axis=2)
    return joined.reshape(SLOTS, 3 * D).astype(jnp.bfloat16)

def reference(tokens, norm_gain, w_qkv, w_out, send_rows, window_rows, grad_out):
    floats = tokens.astype(jnp.float32)
    centred = floats - lax.optimization_barrier(jnp.mean(floats, axis=-1, keepdims=True))
    inv_std = lax.rsqrt(lax.optimization_barrier(jnp.mean(centred * centred, axis=-1, keepdims=True)) + epsilon)
    unit = centred * inv_std
    normed = (unit * norm_gain).astype(jnp.bfloat16)
    packed_all = jnp.dot(normed, w_qkv, preferred_element_type=jnp.float32).astype(jnp.bfloat16)
    slot_ids = slot_tokens(send_rows, window_rows)

    def forward_one(index):
        packed = take_rows(packed_all, index)
        mixed, probs, weights = attend(packed, (index >= 0).reshape(WIN_DEV, WCAP))
        return mixed
    mixed_all = lax.map(forward_one, slot_ids)
    attended = spread_rows(mixed_all.reshape(-1, D), slot_ids.reshape(-1), TOKENS)
    block_out = (floats + jnp.dot(attended, w_out, preferred_element_type=jnp.float32)).astype(jnp.bfloat16)
    grad_w_out = jnp.dot(attended.T, grad_out, preferred_element_type=jnp.float32)
    delta = jnp.dot(grad_out, w_out.T, preferred_element_type=jnp.float32).astype(jnp.bfloat16)

    def backward_one(index):
        packed = take_rows(packed_all, index)
        mixed, probs, weights = attend(packed, (index >= 0).reshape(WIN_DEV, WCAP))
        return attend_back(packed, probs, weights, take_rows(delta, index))
    dpacked_slots = lax.map(backward_one, slot_ids)
    dpacked = spread_rows(dpacked_slots.reshape(-1, 3 * D), slot_ids.reshape(-1), TOKENS)
    grad_w_qkv = jnp.dot(normed.T, dpacked, preferred_element_type=jnp.float32)
    dnormed = jnp.dot(dpacked, w_qkv.T, preferred_element_type=jnp.float32).astype(jnp.bfloat16)
    dnormed_f = dnormed.astype(jnp.float32)
    grad_gain = lax.optimization_barrier(jnp.sum(dnormed_f * unit, axis=0))
    dunit = dnormed_f * norm_gain
    dcentre = inv_std * (dunit - lax.optimization_barrier(jnp.mean(dunit, axis=-1, keepdims=True)) - unit * lax.optimization_barrier(jnp.mean(dunit * unit, axis=-1, keepdims=True)))
    grad_tokens = (grad_out.astype(jnp.float32) + dcentre).astype(jnp.bfloat16)
    return (block_out, grad_tokens, grad_gain, grad_w_qkv, grad_w_out)
```

```python
import functools

import jax
import jax.numpy as jnp
from jax import lax
from jax.experimental import pallas as pl
from jax.experimental.pallas import tpu as pltpu
from jax.sharding import PartitionSpec as P

HEADS = 12
WCAP = 128
COLS = 256
VMEM_BYTES = 56 * 1024 * 1024

epsilon = 1e-06
big_negative = -1e30

AXES = ("gx", "gy", "gz")
MESH = pl.DeviceIdType.MESH
f32 = jnp.float32
bf16 = jnp.bfloat16


def nn(a, b):
    return lax.dot_general(a, b, (((1,), (0,)), ((), ())), preferred_element_type=f32)


def nt(a, b):
    return lax.dot_general(a, b, (((1,), (1,)), ((), ())), preferred_element_type=f32)


def tn(a, b):
    return lax.dot_general(a, b, (((0,), (0,)), ((), ())), preferred_element_type=f32)


def direction(k):
    return (k // 4, k // 2 % 2, k % 2)


def neighbours(sizes):
    here = [lax.axis_index(a) for a in AXES]
    found = []
    for k in range(1, 8):
        step = direction(k)
        up = tuple(here[i] + step[i] for i in range(3))
        down = tuple(here[i] - step[i] for i in range(3))
        has_up = functools.reduce(
            jnp.logical_and, [up[i] < sizes[i] for i in range(3) if step[i]]
        )
        has_down = functools.reduce(
            jnp.logical_and, [down[i] >= 0 for i in range(3) if step[i]]
        )
        found.append((up, down, has_up, has_down))
    return found


def greet(found, partners):
    barrier = pltpu.get_barrier_semaphore()
    count = jnp.int32(len(partners))
    for up, down, has_up, has_down in found:
        @pl.when(has_up)
        def _():
            pl.semaphore_signal(barrier, inc=1, device_id=up, device_id_type=MESH)

        @pl.when(has_down)
        def _():
            pl.semaphore_signal(barrier, inc=1, device_id=down, device_id_type=MESH)

        count = count + has_up.astype(jnp.int32) + has_down.astype(jnp.int32)
    for partner in partners:
        pl.semaphore_signal(barrier, inc=1, device_id=partner, device_id_type=MESH)
    pl.semaphore_wait(barrier, count)


def exchange_kernel(sizes, tok_ref, gout_ref, send_ref, table_ref, buf, send_sem, recv_sem):
    found = neighbours(sizes)
    count, width = tok_ref.shape
    cap = send_ref.shape[0] // 7
    greet(found, [])
    pick = (
        lax.broadcasted_iota(jnp.int32, (7 * cap, count), 1) == send_ref[...]
    ).astype(f32).astype(bf16)
    buf[:, :width] = nn(pick, tok_ref[...]).astype(bf16)
    buf[:, width:] = nn(pick, gout_ref[...]).astype(bf16)

    def copy(k):
        return pltpu.make_async_remote_copy(
            src_ref=buf.at[pl.ds(k * cap, cap)],
            dst_ref=table_ref.at[pl.ds(count + k * cap, cap)],
            send_sem=send_sem.at[k],
            recv_sem=recv_sem.at[k],
            device_id=found[k][0],
            device_id_type=MESH,
        )

    for k in (6, 5, 4, 3, 2, 1, 0):
        @pl.when(found[k][2])
        def _():
            copy(k).start()
    table_ref[:count, :width] = tok_ref[...]
    table_ref[:count, width:] = gout_ref[...]
    for k in range(7):
        @pl.when(jnp.logical_not(found[k][3]))
        def _():
            table_ref[pl.ds(count + k * cap, cap), :] = jnp.zeros((cap, 2 * width), bf16)
    for k in range(7):
        @pl.when(found[k][3])
        def _():
            copy(k).wait_recv()

        @pl.when(found[k][2])
        def _():
            copy(k).wait_send()


def compute_kernel(
    places, table_ref, wcol_ref, wrow_ref, gain_ref, wqkv_ref, wout_ref,
    ret_ref, grad_ref, gsum_ref,
    pick, xs, unit, normed, normed_t, inv, packed, delta, mixed, mixed_t, dpacked, dnormed,
    bg, piece,
):
    span, double = table_ref.shape
    width = double // 2
    slots = wcol_ref.shape[0]
    windows = slots // WCAP
    head_dim = width // HEADS
    scale = head_dim ** (-0.5)

    pick[...] = (
        lax.broadcasted_iota(jnp.int32, (slots, span), 1) == wcol_ref[...]
    ).astype(f32).astype(bf16)

    @pl.loop(0, double // COLS)
    def _(j):
        cols = pl.ds(pl.multiple_of(j * COLS, COLS), COLS)
        xs[:, cols] = nn(pick[...], table_ref[:, cols]).astype(bf16)

    @pl.loop(0, windows)
    def _(w):
        rows = pl.ds(pl.multiple_of(w * WCAP, WCAP), WCAP)
        floats = xs[rows, :width].astype(f32)
        centred = floats - jnp.mean(floats, axis=-1, keepdims=True)
        inv_std = lax.rsqrt(jnp.mean(centred * centred, axis=-1, keepdims=True) + epsilon)
        u = centred * inv_std
        unit[rows, :] = u
        inv[rows, :] = inv_std
        normed[rows, :] = (u * gain_ref[...]).astype(bf16)

    normed_t[...] = normed[...].T

    @pl.loop(0, 3 * width // COLS)
    def _(j):
        cols = pl.ds(pl.multiple_of(j * COLS, COLS), COLS)
        packed[:, cols] = nn(normed[...], wqkv_ref[:, cols]).astype(bf16)

    @pl.loop(0, width // COLS)
    def _(j):
        cols = pl.ds(pl.multiple_of(j * COLS, COLS), COLS)
        delta[:, cols] = nt(xs[:, width:], wout_ref[cols, :]).astype(bf16)

    pair = 2 * head_dim

    @pl.loop(0, windows)
    def _(w):
        rows = pl.ds(pl.multiple_of(w * WCAP, WCAP), WCAP)
        valid = (wcol_ref[rows, :] >= 0)[None]
        first = lax.broadcasted_iota(jnp.int32, (WCAP, pair), 1) < head_dim
        none = jnp.zeros((WCAP, pair), bf16)

        def split(t):
            return jnp.concatenate([jnp.where(first, t, none), jnp.where(first, none, t)], axis=0)

        def join(t):
            return jnp.where(first, t[:WCAP], t[WCAP:])

        for j in range(HEADS // 2):
            at = j * pair
            q = packed[rows, at:at + pair]
            k2 = split(packed[rows, width + at:width + at + pair])
            v2 = split(packed[rows, 2 * width + at:2 * width + at + pair])
            g = delta[rows, at:at + pair]
            scores = nt(k2, q).reshape(2, WCAP, WCAP) * scale
            scores = jnp.where(valid, scores, big_negative)
            top = jnp.max(scores, axis=1, keepdims=True)
            expo = jnp.exp(scores - top)
            probs = expo * (1.0 / jnp.sum(expo, axis=1, keepdims=True))
            weights = probs.reshape(2 * WCAP, WCAP).astype(bf16)
            mixed[rows, at:at + pair] = tn(weights, v2).astype(bf16)
            dweights = nt(v2, g).reshape(2, WCAP, WCAP)
            total = jnp.sum(dweights * probs, axis=1, keepdims=True)
            dscaled = (probs * (dweights - total) * scale).reshape(2 * WCAP, WCAP).astype(bf16)
            dpacked[rows, at:at + pair] = tn(dscaled, k2).astype(bf16)
            dpacked[rows, width + at:width + at + pair] = join(nn(dscaled, q)).astype(bf16)
            dpacked[rows, 2 * width + at:2 * width + at + pair] = join(nn(weights, g)).astype(bf16)

    mixed_t[...] = mixed[...].T

    @pl.loop(0, width // COLS)
    def _(j):
        cols = pl.ds(pl.multiple_of(j * COLS, COLS), COLS)
        out = nn(mixed[...], wout_ref[:, cols])
        bg[:, cols] = (xs[:, cols].astype(f32) + out).astype(bf16)
        dnormed[:, cols] = nt(dpacked[...], wqkv_ref[cols, :]).astype(bf16)

    gsum_ref[...] = jnp.zeros_like(gsum_ref)

    @pl.loop(0, windows)
    def _(w):
        rows = pl.ds(pl.multiple_of(w * WCAP, WCAP), WCAP)
        dn = dnormed[rows, :].astype(f32)
        u = unit[rows, :]
        gsum_ref[...] += jnp.sum((dn * u).reshape(WCAP // 8, 8, width), axis=0)
        dunit = dn * gain_ref[...]
        dcentre = inv[rows, :] * (
            dunit
            - jnp.mean(dunit, axis=-1, keepdims=True)
            - u * jnp.mean(dunit * u, axis=-1, keepdims=True)
        )
        bg[rows, width:] = (xs[rows, width:].astype(f32) + dcentre).astype(bf16)

    back = (
        lax.broadcasted_iota(jnp.int32, (span, slots), 0) == wrow_ref[...]
    ).astype(f32).astype(bf16)
    pick_t = back

    for j in range(double // COLS):
        ret_ref[:, j * COLS:(j + 1) * COLS] = nn(pick_t, bg[:, j * COLS:(j + 1) * COLS]).astype(bf16)

    def gradient(j):
        if j < 3 * width // COLS:
            return nn(normed_t[...], dpacked[:, j * COLS:(j + 1) * COLS])
        at = j * COLS - 3 * width
        return nn(mixed_t[...], xs[:, width + at:width + at + COLS])

    if places is None:
        for j in range(4 * width // COLS):
            grad_ref[:, j * COLS:(j + 1) * COLS] = gradient(j)
        return
    rows = grad_ref.shape[2] // 2
    for p, place in enumerate(places):
        piece[0] = gradient(2 * p)
        piece[1] = gradient(2 * p + 1)
        for c, position in enumerate(place):
            both = jnp.concatenate(
                [piece[0, c * rows:(c + 1) * rows, :], piece[1, c * rows:(c + 1) * rows, :]], axis=0
            )
            grad_ref[p, position] = both.astype(bf16)


def finish_kernel(sizes, orders, bits, *refs):
    parts = len(orders)
    stages = len(bits)
    refs = list(refs)
    ret_ref, srow_ref, gsum_ref = refs[:3]
    refs = refs[3:]
    if parts:
        grad_ref = refs.pop(0)
    block_ref, gtok_ref, gain_ref = refs[:3]
    refs = refs[3:]
    if parts:
        gqkv_ref, gout_ref = refs[:2]
        refs = refs[2:]
    back, gheld, gcome, ret_send, ret_recv, gain_send, gain_recv = refs[:7]
    refs = refs[7:]
    if parts:
        part_send, part_recv = refs[:2]
        come = refs[2:2 + stages]
        held = [grad_ref] + list(refs[2 + stages:])

    found = neighbours(sizes)
    count, width = block_ref.shape
    cap = back.shape[0] // 7
    here = [lax.axis_index(a) for a in AXES]

    def own_bit(bit):
        axis, distance = bit
        return here[axis] // distance % 2

    def partner(bit):
        axis, distance = bit
        return tuple(
            here[i] + distance * (1 - 2 * own_bit(bit)) if i == axis else here[i] for i in range(3)
        )

    greet(found, [partner(bit) for bit in bits])

    def return_copy(k):
        return pltpu.make_async_remote_copy(
            src_ref=ret_ref.at[pl.ds(count + k * cap, cap)],
            dst_ref=back.at[pl.ds(k * cap, cap)],
            send_sem=ret_send.at[k],
            recv_sem=ret_recv.at[k],
            device_id=found[k][1],
            device_id_type=MESH,
        )

    def part_copy(p, s):
        bit = orders[p][s]
        half = come[s].shape[1]
        return pltpu.make_async_remote_copy(
            src_ref=held[s].at[p, pl.ds((1 - own_bit(bit)) * half, half)],
            dst_ref=come[s].at[p],
            send_sem=part_send.at[p * stages + s],
            recv_sem=part_recv.at[p * stages + s],
            device_id=partner(bit),
            device_id_type=MESH,
        )

    def gain_copy(s):
        return pltpu.make_async_remote_copy(
            src_ref=gsum_ref if s == 0 else gheld.at[s - 1],
            dst_ref=gcome.at[s],
            send_sem=gain_send.at[s],
            recv_sem=gain_recv.at[s],
            device_id=partner(bits[s]),
            device_id_type=MESH,
        )

    for p in range(parts):
        part_copy(p, 0).start()
    gain_copy(0).start()
    for k in (6, 5, 4, 3, 2, 1, 0):
        @pl.when(found[k][3])
        def _():
            return_copy(k).start()
    for k in range(7):
        @pl.when(jnp.logical_not(found[k][2]))
        def _():
            back[pl.ds(k * cap, cap), :] = jnp.zeros((cap, 2 * width), bf16)

    for s in range(stages):
        for p in range(parts):
            part_copy(p, s).wait_recv()
            half = come[s].shape[1]
            base = own_bit(orders[p][s]) * half
            if s < stages - 1:
                step = min(half, 2)

                @pl.loop(0, half // step)
                def _(i):
                    mine = held[s][p, pl.ds(base + i * step, step)].astype(f32)
                    theirs = come[s][p, pl.ds(i * step, step)].astype(f32)
                    held[s + 1][p, pl.ds(i * step, step)] = (mine + theirs).astype(bf16)

                part_copy(p, s + 1).start()
            else:
                mine = held[s][p, pl.ds(base, 1)].astype(f32)
                total = mine[0] + come[s][p, 0].astype(f32)
                rows = total.shape[0] // 2
                for i in range(2):
                    at = (2 * p + i) * COLS
                    value = total[i * rows:(i + 1) * rows]
                    if at < 3 * width:
                        gqkv_ref[:, at:at + COLS] = value
                    else:
                        gout_ref[:, at - 3 * width:at - 3 * width + COLS] = value
        gain_copy(s).wait_recv()
        total = (gsum_ref[...] if s == 0 else gheld[s - 1]) + gcome[s]
        if s < stages - 1:
            gheld[s] = total
            gain_copy(s + 1).start()
        else:
            gain_ref[...] = total

    for k in range(7):
        @pl.when(found[k][2])
        def _():
            return_copy(k).wait_recv()
    place = (
        lax.broadcasted_iota(jnp.int32, (count, 7 * cap), 0) == srow_ref[...]
    ).astype(f32).astype(bf16)
    block_ref[...] = (
        ret_ref[:count, :width].astype(f32) + nn(place, back[:, :width])
    ).astype(bf16)
    gtok_ref[...] = (
        ret_ref[:count, width:].astype(f32) + nn(place, back[:, width:])
    ).astype(bf16)

    for k in range(7):
        @pl.when(found[k][3])
        def _():
            return_copy(k).wait_send()
    for s in range(stages):
        for p in range(parts):
            part_copy(p, s).wait_send()
        gain_copy(s).wait_send()


def on_device(sizes, tokens, norm_gain, w_qkv, w_out, send_rows, window_rows, grad_out):
    count, width = tokens.shape
    slots = window_rows.shape[1]
    cap = send_rows.shape[2]
    span = count + 7 * cap
    devices = sizes[0] * sizes[1] * sizes[2]
    vmem = pl.BlockSpec(memory_space=pltpu.VMEM)
    params = functools.partial(pltpu.CompilerParams, vmem_limit_bytes=VMEM_BYTES)

    by_axis = [[(a, 1 << i) for i in range(sizes[a].bit_length() - 1)] for a in range(3)]
    x_bits, y_bits, z_bits = by_axis
    bits = y_bits + x_bits + z_bits
    chunk = width // devices
    grouped = (
        all(1 << len(b) == n for b, n in zip(by_axis, sizes))
        and len(y_bits) > 0
        and chunk * devices == width
        and chunk % 8 == 0
    )
    parts = 4 * width // (2 * COLS)
    orders, places = [], None
    if grouped:
        rest = y_bits[1:]
        kinds = [
            y_bits[:1] + x_bits + rest + z_bits,
            y_bits[:1] + rest + z_bits + x_bits,
            y_bits[:1] + z_bits + x_bits + rest,
        ]
        orders = [kinds[p % 3] for p in range(parts)]

        def position(order, c):
            at = (c // (sizes[1] * sizes[2]), c // sizes[2] % sizes[1], c % sizes[2])
            value = 0
            for axis, distance in order:
                value = 2 * value + at[axis] // distance % 2
            return value

        places = [[position(order, c) for c in range(devices)] for order in orders]

    send_flat = send_rows.reshape(7 * cap)
    send_col = send_flat.reshape(7 * cap, 1)
    send_row = send_flat.reshape(1, 7 * cap)
    slot_col = window_rows.reshape(slots, 1)

    table = pl.pallas_call(
        functools.partial(exchange_kernel, sizes),
        out_shape=jax.ShapeDtypeStruct((span, 2 * width), bf16),
        in_specs=[vmem] * 3,
        out_specs=vmem,
        scratch_shapes=[
            pltpu.VMEM((7 * cap, 2 * width), bf16),
            pltpu.SemaphoreType.DMA((7,)),
            pltpu.SemaphoreType.DMA((7,)),
        ],
        compiler_params=params(collective_id=0, has_side_effects=True),
        name="exchange",
    )(tokens, grad_out, send_col)

    if grouped:
        grad_shape = jax.ShapeDtypeStruct((parts, devices, 2 * chunk, COLS), bf16)
    else:
        grad_shape = jax.ShapeDtypeStruct((width, 4 * width), f32)
    ret, grads, gsum = pl.pallas_call(
        functools.partial(compute_kernel, places),
        out_shape=(
            jax.ShapeDtypeStruct((span, 2 * width), bf16),
            grad_shape,
            jax.ShapeDtypeStruct((8, width), f32),
        ),
        in_specs=[vmem] * 6,
        out_specs=(vmem,) * 3,
        scratch_shapes=[
            pltpu.VMEM((slots, span), bf16),
            pltpu.VMEM((slots, 2 * width), bf16),
            pltpu.VMEM((slots, width), f32),
            pltpu.VMEM((slots, width), bf16),
            pltpu.VMEM((width, slots), bf16),
            pltpu.VMEM((slots, 1), f32),
            pltpu.VMEM((slots, 3 * width), bf16),
            pltpu.VMEM((slots, width), bf16),
            pltpu.VMEM((slots, width), bf16),
            pltpu.VMEM((width, slots), bf16),
            pltpu.VMEM((slots, 3 * width), bf16),
            pltpu.VMEM((slots, width), bf16),
            pltpu.VMEM((slots, 2 * width), bf16),
            pltpu.VMEM((2, width, COLS), f32),
        ],
        compiler_params=params(),
        name="windows",
    )(table, slot_col, window_rows, norm_gain.reshape(1, width), w_qkv, w_out)

    stages = len(bits)
    out_shape = [
        jax.ShapeDtypeStruct((count, width), bf16),
        jax.ShapeDtypeStruct((count, width), bf16),
        jax.ShapeDtypeStruct((8, width), f32),
    ]
    scratch = [
        pltpu.VMEM((7 * cap, 2 * width), bf16),
        pltpu.VMEM((stages, 8, width), f32),
        pltpu.VMEM((stages, 8, width), f32),
        pltpu.SemaphoreType.DMA((7,)),
        pltpu.SemaphoreType.DMA((7,)),
        pltpu.SemaphoreType.DMA((stages,)),
        pltpu.SemaphoreType.DMA((stages,)),
    ]
    operands = [ret, send_row, gsum]
    if grouped:
        out_shape += [
            jax.ShapeDtypeStruct((chunk, 3 * width), f32),
            jax.ShapeDtypeStruct((chunk, width), f32),
        ]
        scratch += [pltpu.SemaphoreType.DMA((parts * stages,))] * 2
        slab = (2 * chunk, COLS)
        scratch += [pltpu.VMEM((parts, devices >> (s + 1)) + slab, bf16) for s in range(stages)]
        scratch += [pltpu.VMEM((parts, devices >> s) + slab, bf16) for s in range(1, stages)]
        operands.append(grads)
    outs = pl.pallas_call(
        functools.partial(finish_kernel, sizes, orders, bits),
        out_shape=tuple(out_shape),
        in_specs=[vmem] * len(operands),
        out_specs=(vmem,) * len(out_shape),
        scratch_shapes=scratch,
        compiler_params=params(collective_id=1, has_side_effects=True),
        name="finish",
    )(*operands)
    block_out, grad_tokens, gain_sum = outs[:3]
    me = (lax.axis_index("gx") * sizes[1] + lax.axis_index("gy")) * sizes[2] + lax.axis_index("gz")
    grad_gain = jnp.sum(lax.dynamic_slice_in_dim(gain_sum, me * chunk, chunk, axis=1), axis=0)
    if grouped:
        grad_qkv, grad_proj = outs[3:]
    else:
        summed = lax.psum_scatter(grads, AXES, scatter_dimension=0, tiled=True)
        grad_qkv, grad_proj = summed[:, :3 * width], summed[:, 3 * width:]
    return (block_out, grad_tokens, grad_gain, grad_qkv, grad_proj)


def solution(mesh):
    sizes = tuple(mesh.shape[a] for a in AXES)
    in_specs = (
        P(AXES, None),
        P(),
        P(),
        P(),
        P(AXES, None, None),
        P(AXES, None),
        P(AXES, None),
    )
    out_specs = (
        P(AXES, None),
        P(AXES, None),
        P(AXES),
        P(AXES, None),
        P(AXES, None),
    )
    return jax.shard_map(
        functools.partial(on_device, sizes),
        mesh=mesh,
        in_specs=in_specs,
        out_specs=out_specs,
        check_vma=False,
    )
```

```python
import functools

import jax
import jax.numpy as jnp
from jax import lax
from jax.experimental import pallas as pl
from jax.experimental.pallas import tpu as pltpu
from jax.sharding import PartitionSpec as P

HEADS = 12
WCAP = 128
COLS = 256
HALF = 128
VMEM_BYTES = 56 * 1024 * 1024

epsilon = 1e-06
big_negative = -1e30

AXES = ("gx", "gy", "gz")
MESH = pl.DeviceIdType.MESH
f32 = jnp.float32
bf16 = jnp.bfloat16


def nn(a, b):
    return lax.dot_general(a, b, (((1,), (0,)), ((), ())), preferred_element_type=f32)


def nt(a, b):
    return lax.dot_general(a, b, (((1,), (1,)), ((), ())), preferred_element_type=f32)


def tn(a, b):
    return lax.dot_general(a, b, (((0,), (0,)), ((), ())), preferred_element_type=f32)


def direction(k):
    return (k // 4, k // 2 % 2, k % 2)


def neighbours(sizes):
    here = [lax.axis_index(a) for a in AXES]
    found = []
    for k in range(1, 8):
        step = direction(k)
        up = tuple(here[i] + step[i] for i in range(3))
        down = tuple(here[i] - step[i] for i in range(3))
        has_up = functools.reduce(
            jnp.logical_and, [up[i] < sizes[i] for i in range(3) if step[i]]
        )
        has_down = functools.reduce(
            jnp.logical_and, [down[i] >= 0 for i in range(3) if step[i]]
        )
        found.append((up, down, has_up, has_down))
    return found


def greet(found, partners):
    barrier = pltpu.get_barrier_semaphore()
    count = jnp.int32(len(partners))
    for up, down, has_up, has_down in found:
        @pl.when(has_up)
        def _():
            pl.semaphore_signal(barrier, inc=1, device_id=up, device_id_type=MESH)

        @pl.when(has_down)
        def _():
            pl.semaphore_signal(barrier, inc=1, device_id=down, device_id_type=MESH)

        count = count + has_up.astype(jnp.int32) + has_down.astype(jnp.int32)
    for partner in partners:
        pl.semaphore_signal(barrier, inc=1, device_id=partner, device_id_type=MESH)
    pl.semaphore_wait(barrier, count)


def block_kernel(sizes, orders, bits, places, *refs):
    parts, stages = len(orders), len(bits)
    refs = list(refs)

    def take(n):
        out = refs[:n]
        del refs[:n]
        return out

    tok_ref, gout_ref, send_ref, wrow_ref, gain_ref, wqkv_hbm, wout_hbm = take(7)
    own_ref, back_ref, place_ref, gsum_ref = take(4)
    if parts:
        gqkv_ref, gproj_ref = take(2)
    else:
        (grad_ref,) = take(1)
    buf, table, wqkv_ref, wout_ref, wcol, pick = take(6)
    xs, unit, normed, normed_t, inv, packed, delta, mixed, mixed_t, dpacked, dnormed = take(11)
    bg, ret = take(2)
    gheld, gcome = take(2)
    load_sem, send_sem, recv_sem, ret_send, ret_recv, gain_send, gain_recv = take(7)
    if parts:
        piece, part_send, part_recv = take(3)
        come = take(stages)
        held = take(stages)

    found = neighbours(sizes)
    count, width = tok_ref.shape
    double = 2 * width
    cap = send_ref.shape[2]
    span = count + 7 * cap
    slots = wrow_ref.shape[1]
    windows = slots // WCAP
    head_dim = width // HEADS
    pair = 2 * head_dim
    scale = head_dim ** (-0.5)
    here = [lax.axis_index(a) for a in AXES]

    def own_bit(bit):
        axis, distance = bit
        return here[axis] // distance % 2

    def partner(bit):
        axis, distance = bit
        return tuple(
            here[i] + distance * (1 - 2 * own_bit(bit)) if i == axis else here[i] for i in range(3)
        )

    def forward_copy(k):
        return pltpu.make_async_remote_copy(
            src_ref=buf.at[pl.ds(k * cap, cap)],
            dst_ref=table.at[pl.ds(count + k * cap, cap)],
            send_sem=send_sem.at[k],
            recv_sem=recv_sem.at[k],
            device_id=found[k][0],
            device_id_type=MESH,
        )

    def return_copy(k):
        return pltpu.make_async_remote_copy(
            src_ref=ret.at[pl.ds(k * cap, cap)],
            dst_ref=back_ref.at[pl.ds(k * cap, cap)],
            send_sem=ret_send.at[k],
            recv_sem=ret_recv.at[k],
            device_id=found[k][1],
            device_id_type=MESH,
        )

    def part_copy(p, s):
        bit = orders[p][s]
        half = come[s].shape[1]
        return pltpu.make_async_remote_copy(
            src_ref=held[s].at[p, pl.ds((1 - own_bit(bit)) * half, half)],
            dst_ref=come[s].at[p],
            send_sem=part_send.at[p * stages + s],
            recv_sem=part_recv.at[p * stages + s],
            device_id=partner(bit),
            device_id_type=MESH,
        )

    def gain_copy(s):
        return pltpu.make_async_remote_copy(
            src_ref=gheld.at[s],
            dst_ref=gcome.at[s],
            send_sem=gain_send.at[s],
            recv_sem=gain_recv.at[s],
            device_id=partner(bits[s]),
            device_id_type=MESH,
        )

    loads = [
        pltpu.make_async_copy(wqkv_hbm, wqkv_ref, load_sem.at[0]),
        pltpu.make_async_copy(wout_hbm, wout_ref, load_sem.at[1]),
    ]
    for load in loads:
        load.start()

    send_row = jnp.concatenate([send_ref[0, k:k + 1, :] for k in range(7)], axis=1)
    place = (
        lax.broadcasted_iota(jnp.int32, (count, 7 * cap), 0) == send_row
    ).astype(f32).astype(bf16)
    place_ref[...] = place
    buf[:, :width] = tn(place, tok_ref[...]).astype(bf16)
    buf[:, width:] = tn(place, gout_ref[...]).astype(bf16)
    greet(found, [partner(bit) for bit in bits])
    for k in (6, 5, 4, 3, 2, 1, 0):
        @pl.when(found[k][2])
        def _():
            forward_copy(k).start()
    table[:count, :width] = tok_ref[...]
    table[:count, width:] = gout_ref[...]
    for k in range(7):
        @pl.when(jnp.logical_not(found[k][3]))
        def _():
            table[pl.ds(count + k * cap, cap), :] = jnp.zeros((cap, double), bf16)

        @pl.when(jnp.logical_not(found[k][2]))
        def _():
            back_ref[pl.ds(k * cap, cap), :] = jnp.zeros((cap, double), bf16)
    wcol[...] = jnp.broadcast_to(wrow_ref[...], (8, slots)).T[:, :1]
    pick[...] = (
        lax.broadcasted_iota(jnp.int32, (slots, span), 1) == wcol[...]
    ).astype(f32).astype(bf16)
    gain_row = gain_ref[...].reshape(1, width)
    for load in loads:
        load.wait()
    for k in range(7):
        @pl.when(found[k][3])
        def _():
            forward_copy(k).wait_recv()

        @pl.when(found[k][2])
        def _():
            forward_copy(k).wait_send()

    @pl.loop(0, double // COLS)
    def _(j):
        cols = pl.ds(pl.multiple_of(j * COLS, COLS), COLS)
        xs[:, cols] = nn(pick[...], table[:, cols]).astype(bf16)

    @pl.loop(0, windows)
    def _(w):
        rows = pl.ds(pl.multiple_of(w * WCAP, WCAP), WCAP)
        floats = xs[rows, :width].astype(f32)
        centred = floats - jnp.mean(floats, axis=-1, keepdims=True)
        inv_std = lax.rsqrt(jnp.mean(centred * centred, axis=-1, keepdims=True) + epsilon)
        u = centred * inv_std
        unit[rows, :] = u
        inv[rows, :] = inv_std
        normed[rows, :] = (u * gain_row).astype(bf16)

    normed_t[...] = normed[...].T

    @pl.loop(0, 3 * width // COLS)
    def _(j):
        cols = pl.ds(pl.multiple_of(j * COLS, COLS), COLS)
        packed[:, cols] = nn(normed[...], wqkv_ref[:, cols]).astype(bf16)

    @pl.loop(0, width // COLS)
    def _(j):
        cols = pl.ds(pl.multiple_of(j * COLS, COLS), COLS)
        delta[:, cols] = nt(xs[:, width:], wout_ref[cols, :]).astype(bf16)

    def attention(group):
        @pl.loop(0, windows)
        def _(w):
            rows = pl.ds(pl.multiple_of(w * WCAP, WCAP), WCAP)
            valid = (wcol[rows, :] >= 0)[None]
            first = lax.broadcasted_iota(jnp.int32, (WCAP, pair), 1) < head_dim
            none = jnp.zeros((WCAP, pair), bf16)

            def split(t):
                return jnp.concatenate(
                    [jnp.where(first, t, none), jnp.where(first, none, t)], axis=0
                )

            def join(t):
                return jnp.where(first, t[:WCAP], t[WCAP:])

            for j in (2 * group, 2 * group + 1):
                at = j * pair
                q = packed[rows, at:at + pair]
                k2 = split(packed[rows, width + at:width + at + pair])
                v2 = split(packed[rows, 2 * width + at:2 * width + at + pair])
                g = delta[rows, at:at + pair]
                scores = nt(k2, q).reshape(2, WCAP, WCAP) * scale
                scores = jnp.where(valid, scores, big_negative)
                top = jnp.max(scores, axis=1, keepdims=True)
                expo = jnp.exp(scores - top)
                probs = expo * (1.0 / jnp.sum(expo, axis=1, keepdims=True))
                weights = probs.reshape(2 * WCAP, WCAP).astype(bf16)
                mixed[rows, at:at + pair] = tn(weights, v2).astype(bf16)
                dweights = nt(v2, g).reshape(2, WCAP, WCAP)
                total = jnp.sum(dweights * probs, axis=1, keepdims=True)
                dscaled = (probs * (dweights - total) * scale).reshape(2 * WCAP, WCAP).astype(bf16)
                dpacked[rows, at:at + pair] = tn(dscaled, k2).astype(bf16)
                dpacked[rows, width + at:width + at + pair] = join(nn(dscaled, q)).astype(bf16)
                dpacked[rows, 2 * width + at:2 * width + at + pair] = join(
                    nn(weights, g)
                ).astype(bf16)

    def first_column(p):
        return (p % 3) * width + (p // 3) * COLS if p < parts - 3 else 3 * width + (p - parts + 3) * COLS

    def gradient(at):
        if at < 3 * width:
            return nn(normed_t[...], dpacked[:, at:at + COLS])
        return nn(mixed_t[...], xs[:, at - 2 * width:at - 2 * width + COLS])

    def open_parts(members):
        for p in members:
            piece[p % 2] = gradient(first_column(p))
            rows = held[0].shape[2] // 2
            for c, position in enumerate(places[p]):
                both = piece[p % 2, c * rows:(c + 1) * rows, :]
                held[0][p, position] = jnp.concatenate(
                    [both[:, :HALF], both[:, HALF:]], axis=0
                ).astype(bf16)
            part_copy(p, 0).start()

    def advance(members, s):
        for p in members:
            part_copy(p, s).wait_recv()
            half = come[s].shape[1]
            base = own_bit(orders[p][s]) * half
            if s < stages - 1:
                step = min(half, 4)

                @pl.loop(0, half // step)
                def _(i):
                    mine = held[s][p, pl.ds(base + i * step, step)].astype(f32)
                    theirs = come[s][p, pl.ds(i * step, step)].astype(f32)
                    held[s + 1][p, pl.ds(i * step, step)] = (mine + theirs).astype(bf16)

                part_copy(p, s + 1).start()
            else:
                mine = held[s][p, pl.ds(base, 1)].astype(f32)
                total = mine[0] + come[s][p, 0].astype(f32)
                rows = total.shape[0] // 2
                for i in range(2):
                    at = first_column(p) + i * HALF
                    value = total[i * rows:(i + 1) * rows]
                    if at < 3 * width:
                        gqkv_ref[:, at:at + HALF] = value
                    else:
                        gproj_ref[:, at - 3 * width:at - 3 * width + HALF] = value

    def advance_gain(s):
        gain_copy(s).wait_recv()
        total = gheld[s] + gcome[s]
        if s < stages - 1:
            gheld[s + 1] = total
            gain_copy(s + 1).start()
        else:
            gsum_ref[...] = total

    groups = HEADS // 4
    waves = [range(3 * i, 3 * i + 3) for i in range(parts // 3)]
    for group in range(groups):
        attention(group)
        if parts:
            open_parts(waves[group])
            for i in range(group):
                advance(waves[i], group - 1 - i)

    mixed_t[...] = mixed[...].T
    if parts:
        open_parts(waves[groups])
        for i in range(groups):
            advance(waves[i], groups - 1 - i)

    @pl.loop(0, width // COLS)
    def _(j):
        cols = pl.ds(pl.multiple_of(j * COLS, COLS), COLS)
        out = nn(mixed[...], wout_ref[:, cols])
        bg[:, cols] = (xs[:, cols].astype(f32) + out).astype(bf16)
        dnormed[:, cols] = nt(dpacked[...], wqkv_ref[cols, :]).astype(bf16)

    gheld[0] = jnp.zeros((8, width), f32)

    @pl.loop(0, windows)
    def _(w):
        rows = pl.ds(pl.multiple_of(w * WCAP, WCAP), WCAP)
        dn = dnormed[rows, :].astype(f32)
        u = unit[rows, :]
        gheld[0] += jnp.sum((dn * u).reshape(WCAP // 8, 8, width), axis=0)
        dunit = dn * gain_row
        dcentre = inv[rows, :] * (
            dunit
            - jnp.mean(dunit, axis=-1, keepdims=True)
            - u * jnp.mean(dunit * u, axis=-1, keepdims=True)
        )
        bg[rows, width:] = (xs[rows, width:].astype(f32) + dcentre).astype(bf16)

    gain_copy(0).start()
    received = (
        lax.broadcasted_iota(jnp.int32, (7 * cap, slots), 0) + count == wrow_ref[...]
    ).astype(f32).astype(bf16)
    for j in range(double // COLS):
        cols = slice(j * COLS, (j + 1) * COLS)
        ret[:, cols] = nn(received, bg[:, cols]).astype(bf16)
    for k in (6, 5, 4, 3, 2, 1, 0):
        @pl.when(found[k][3])
        def _():
            return_copy(k).start()
    kept = (
        lax.broadcasted_iota(jnp.int32, (count, slots), 0) == wrow_ref[...]
    ).astype(f32).astype(bf16)
    for j in range(double // COLS):
        cols = slice(j * COLS, (j + 1) * COLS)
        own_ref[:, cols] = nn(kept, bg[:, cols]).astype(bf16)

    if not parts:
        for j in range(4 * width // COLS):
            grad_ref[:, j * COLS:(j + 1) * COLS] = gradient(j * COLS)
    for turn in range(groups, stages + groups):
        for i in range(len(waves)):
            if 0 <= turn - i < stages:
                advance(waves[i], turn - i)
        if turn - groups < stages:
            advance_gain(turn - groups)

    for k in range(7):
        @pl.when(found[k][2])
        def _():
            return_copy(k).wait_recv()

        @pl.when(found[k][3])
        def _():
            return_copy(k).wait_send()
    for s in range(stages):
        for p in range(parts):
            part_copy(p, s).wait_send()
        gain_copy(s).wait_send()


def finish_kernel(own_ref, back_ref, place_ref, *refs):
    many = len(refs) // 2 - 1
    given, (block_ref, gtok_ref, *final) = refs[:many], refs[many:]
    width = block_ref.shape[1]
    place = place_ref[...]
    block_ref[...] = (
        own_ref[:, :width].astype(f32) + nn(place, back_ref[:, :width])
    ).astype(bf16)
    gtok_ref[...] = (
        own_ref[:, width:].astype(f32) + nn(place, back_ref[:, width:])
    ).astype(bf16)
    for source, target in zip(given, final):
        target[...] = source[...]


def on_device(sizes, tokens, norm_gain, w_qkv, w_out, send_rows, window_rows, grad_out):
    count, width = tokens.shape
    slots = window_rows.shape[1]
    cap = send_rows.shape[2]
    span = count + 7 * cap
    devices = sizes[0] * sizes[1] * sizes[2]
    vmem = pl.BlockSpec(memory_space=pltpu.VMEM)
    params = functools.partial(pltpu.CompilerParams, vmem_limit_bytes=VMEM_BYTES)

    by_axis = [[(a, 1 << i) for i in range(sizes[a].bit_length() - 1)] for a in range(3)]
    x_bits, y_bits, z_bits = by_axis
    bits = y_bits + x_bits + z_bits
    chunk = width // devices
    grouped = (
        all(1 << len(b) == n for b, n in zip(by_axis, sizes))
        and len(y_bits) > 0
        and chunk * devices == width
        and chunk % 8 == 0
    )
    parts = 4 * width // COLS
    orders, places = [], None
    if grouped:
        rest = y_bits[1:]
        kinds = [
            y_bits[:1] + x_bits + rest + z_bits,
            y_bits[:1] + rest + z_bits + x_bits,
            y_bits[:1] + z_bits + x_bits + rest,
        ]
        orders = [kinds[p % 3] for p in range(parts)]

        def position(order, c):
            at = (c // (sizes[1] * sizes[2]), c // sizes[2] % sizes[1], c % sizes[2])
            value = 0
            for axis, distance in order:
                value = 2 * value + at[axis] // distance % 2
            return value

        places = [[position(order, c) for c in range(devices)] for order in orders]

    stages = len(bits)
    anywhere = pl.BlockSpec(memory_space=pl.ANY)
    out_shape = [
        jax.ShapeDtypeStruct((count, 2 * width), bf16),
        jax.ShapeDtypeStruct((7 * cap, 2 * width), bf16),
        jax.ShapeDtypeStruct((count, 7 * cap), bf16),
        jax.ShapeDtypeStruct((8, width), f32),
    ]
    if grouped:
        sums = [
            jax.ShapeDtypeStruct((chunk, 3 * width), f32),
            jax.ShapeDtypeStruct((chunk, width), f32),
        ]
    else:
        sums = [jax.ShapeDtypeStruct((width, 4 * width), f32)]
    scratch = [
        pltpu.VMEM((7 * cap, 2 * width), bf16),
        pltpu.VMEM((span, 2 * width), bf16),
        pltpu.VMEM((width, 3 * width), bf16),
        pltpu.VMEM((width, width), bf16),
        pltpu.VMEM((slots, 1), jnp.int32),
        pltpu.VMEM((slots, span), bf16),
        pltpu.VMEM((slots, 2 * width), bf16),
        pltpu.VMEM((slots, width), f32),
        pltpu.VMEM((slots, width), bf16),
        pltpu.VMEM((width, slots), bf16),
        pltpu.VMEM((slots, 1), f32),
        pltpu.VMEM((slots, 3 * width), bf16),
        pltpu.VMEM((slots, width), bf16),
        pltpu.VMEM((slots, width), bf16),
        pltpu.VMEM((width, slots), bf16),
        pltpu.VMEM((slots, 3 * width), bf16),
        pltpu.VMEM((slots, width), bf16),
        pltpu.VMEM((slots, 2 * width), bf16),
        pltpu.VMEM((7 * cap, 2 * width), bf16),
        pltpu.VMEM((stages, 8, width), f32),
        pltpu.VMEM((stages, 8, width), f32),
        pltpu.SemaphoreType.DMA((2,)),
        pltpu.SemaphoreType.DMA((7,)),
        pltpu.SemaphoreType.DMA((7,)),
        pltpu.SemaphoreType.DMA((7,)),
        pltpu.SemaphoreType.DMA((7,)),
        pltpu.SemaphoreType.DMA((stages,)),
        pltpu.SemaphoreType.DMA((stages,)),
    ]
    if grouped:
        slab = (2 * chunk, HALF)
        scratch += [pltpu.VMEM((2, width, COLS), f32)]
        scratch += [pltpu.SemaphoreType.DMA((parts * stages,))] * 2
        scratch += [pltpu.VMEM((parts, devices >> (s + 1)) + slab, bf16) for s in range(stages)]
        scratch += [pltpu.VMEM((parts, devices >> s) + slab, bf16) for s in range(stages)]
    own, back, place, gain_sum, *grads = pl.pallas_call(
        functools.partial(block_kernel, sizes, orders, bits, places),
        out_shape=tuple(out_shape + sums),
        in_specs=[vmem] * 5 + [anywhere] * 2,
        out_specs=(vmem,) * len(out_shape + sums),
        scratch_shapes=scratch,
        compiler_params=params(collective_id=0, has_side_effects=True),
        name="block",
    )(tokens, grad_out, send_rows, window_rows, norm_gain, w_qkv, w_out)

    passed = grads if grouped else []
    final_shape = [jax.ShapeDtypeStruct((count, width), bf16)] * 2 + (sums if grouped else [])
    block_out, grad_tokens, *final = pl.pallas_call(
        finish_kernel,
        out_shape=tuple(final_shape),
        in_specs=[vmem] * (3 + len(passed)),
        out_specs=(vmem,) * len(final_shape),
        compiler_params=params(),
        name="finish",
    )(own, back, place, *passed)
    me = (lax.axis_index("gx") * sizes[1] + lax.axis_index("gy")) * sizes[2] + lax.axis_index("gz")
    grad_gain = jnp.sum(lax.dynamic_slice_in_dim(gain_sum, me * chunk, chunk, axis=1), axis=0)
    if grouped:
        grad_qkv, grad_proj = final
    else:
        summed = lax.psum_scatter(grads[0], AXES, scatter_dimension=0, tiled=True)
        grad_qkv, grad_proj = summed[:, :3 * width], summed[:, 3 * width:]
    return (block_out, grad_tokens, grad_gain, grad_qkv, grad_proj)


def solution(mesh):
    sizes = tuple(mesh.shape[a] for a in AXES)
    in_specs = (
        P(AXES, None),
        P(),
        P(),
        P(),
        P(AXES, None, None),
        P(AXES, None),
        P(AXES, None),
    )
    out_specs = (
        P(AXES, None),
        P(AXES, None),
        P(AXES),
        P(AXES, None),
        P(AXES, None),
    )
    return jax.shard_map(
        functools.partial(on_device, sizes),
        mesh=mesh,
        in_specs=in_specs,
        out_specs=out_specs,
        check_vma=False,
    )
```

```python
import functools

import jax
import jax.numpy as jnp
from jax import lax
from jax.experimental import pallas as pl
from jax.experimental.pallas import tpu as pltpu
from jax.sharding import PartitionSpec as P

HEADS = 12
WCAP = 128
COLS = 256
HALF = 128
PLAN = (0, 1, 2, 0, 1, 0, 1, 0, 1, 2, 1, 0)
VMEM_BYTES = 56 * 1024 * 1024

epsilon = 1e-06
big_negative = -1e30

AXES = ("gx", "gy", "gz")
MESH = pl.DeviceIdType.MESH
f32 = jnp.float32
bf16 = jnp.bfloat16


def nn(a, b):
    return lax.dot_general(a, b, (((1,), (0,)), ((), ())), preferred_element_type=f32)


def nt(a, b):
    return lax.dot_general(a, b, (((1,), (1,)), ((), ())), preferred_element_type=f32)


def tn(a, b):
    return lax.dot_general(a, b, (((0,), (0,)), ((), ())), preferred_element_type=f32)


def direction(k):
    return (k // 4, k // 2 % 2, k % 2)


def neighbours(sizes):
    here = [lax.axis_index(a) for a in AXES]
    found = []
    for k in range(1, 8):
        step = direction(k)
        up = tuple(here[i] + step[i] for i in range(3))
        down = tuple(here[i] - step[i] for i in range(3))
        has_up = functools.reduce(
            jnp.logical_and, [up[i] < sizes[i] for i in range(3) if step[i]]
        )
        has_down = functools.reduce(
            jnp.logical_and, [down[i] >= 0 for i in range(3) if step[i]]
        )
        found.append((up, down, has_up, has_down))
    return found


def greet(found, partners):
    barrier = pltpu.get_barrier_semaphore()
    count = jnp.int32(len(partners))
    for up, down, has_up, has_down in found:
        @pl.when(has_up)
        def _():
            pl.semaphore_signal(barrier, inc=1, device_id=up, device_id_type=MESH)

        @pl.when(has_down)
        def _():
            pl.semaphore_signal(barrier, inc=1, device_id=down, device_id_type=MESH)

        count = count + has_up.astype(jnp.int32) + has_down.astype(jnp.int32)
    for partner in partners:
        pl.semaphore_signal(barrier, inc=1, device_id=partner, device_id_type=MESH)
    pl.semaphore_wait(barrier, count)


def block_kernel(sizes, orders, bits, places, *refs):
    parts, stages = len(orders), len(bits)
    refs = list(refs)

    def take(n):
        out = refs[:n]
        del refs[:n]
        return out

    tok_ref, gout_ref, send_ref, wrow_ref, gain_ref, wqkv_hbm, wout_hbm = take(7)
    own_ref, back_ref, place_ref, gsum_ref = take(4)
    if parts:
        gqkv_ref, gproj_ref = take(2)
    else:
        (grad_ref,) = take(1)
    buf, table, wqkv_ref, wout_ref, wcol, pick = take(6)
    xs, unit, normed, normed_t, inv, packed, delta, mixed, mixed_t, dpacked, dnormed = take(11)
    bg, ret = take(2)
    gheld, gcome = take(2)
    load_sem, send_sem, recv_sem, ret_send, ret_recv, gain_send, gain_recv = take(7)
    if parts:
        piece, part_send, part_recv = take(3)
        come = take(stages)
        held = take(stages)

    found = neighbours(sizes)
    count, width = tok_ref.shape
    double = 2 * width
    cap = send_ref.shape[2]
    span = count + 7 * cap
    slots = wrow_ref.shape[1]
    windows = slots // WCAP
    head_dim = width // HEADS
    pair = 2 * head_dim
    scale = head_dim ** (-0.5)
    here = [lax.axis_index(a) for a in AXES]

    def own_bit(bit):
        axis, distance = bit
        return here[axis] // distance % 2

    def partner(bit):
        axis, distance = bit
        return tuple(
            here[i] + distance * (1 - 2 * own_bit(bit)) if i == axis else here[i] for i in range(3)
        )

    def forward_copy(h, k):
        return pltpu.make_async_remote_copy(
            src_ref=buf.at[h, pl.ds(k * cap, cap)],
            dst_ref=table.at[h, pl.ds(k * cap, cap)],
            send_sem=send_sem.at[7 * h + k],
            recv_sem=recv_sem.at[7 * h + k],
            device_id=found[k][0],
            device_id_type=MESH,
        )

    def return_copy(k):
        return pltpu.make_async_remote_copy(
            src_ref=ret.at[pl.ds(k * cap, cap)],
            dst_ref=back_ref.at[pl.ds(k * cap, cap)],
            send_sem=ret_send.at[k],
            recv_sem=ret_recv.at[k],
            device_id=found[k][1],
            device_id_type=MESH,
        )

    def part_copy(p, s):
        bit = orders[p][s]
        half = come[s].shape[1]
        return pltpu.make_async_remote_copy(
            src_ref=held[s].at[p, pl.ds((1 - own_bit(bit)) * half, half)],
            dst_ref=come[s].at[p],
            send_sem=part_send.at[p * stages + s],
            recv_sem=part_recv.at[p * stages + s],
            device_id=partner(bit),
            device_id_type=MESH,
        )

    def gain_copy(s):
        return pltpu.make_async_remote_copy(
            src_ref=gheld.at[s],
            dst_ref=gcome.at[s],
            send_sem=gain_send.at[s],
            recv_sem=gain_recv.at[s],
            device_id=partner(bits[s]),
            device_id_type=MESH,
        )

    loads = [
        pltpu.make_async_copy(wqkv_hbm, wqkv_ref, load_sem.at[0]),
        pltpu.make_async_copy(wout_hbm, wout_ref, load_sem.at[1]),
    ]
    for load in loads:
        load.start()

    send_row = jnp.concatenate([send_ref[k] for k in range(7)], axis=1)
    place = (
        lax.broadcasted_iota(jnp.int32, (count, 7 * cap), 0) == send_row
    ).astype(f32).astype(bf16)
    place_ref[...] = place
    buf[0] = tn(place, tok_ref[...]).astype(bf16)
    greet(found, [partner(bit) for bit in bits])

    def start_forward(h):
        for k in (6, 5, 4, 3, 2, 1, 0):
            @pl.when(found[k][2])
            def _():
                forward_copy(h, k).start()

    def wait_forward(h):
        for k in range(7):
            @pl.when(found[k][3])
            def _():
                forward_copy(h, k).wait_recv()

            @pl.when(found[k][2])
            def _():
                forward_copy(h, k).wait_send()

    start_forward(0)
    buf[1] = tn(place, gout_ref[...]).astype(bf16)
    start_forward(1)
    for k in range(7):
        @pl.when(jnp.logical_not(found[k][3]))
        def _():
            for h in range(2):
                table[h, pl.ds(k * cap, cap), :] = jnp.zeros((cap, width), bf16)

        @pl.when(jnp.logical_not(found[k][2]))
        def _():
            back_ref[pl.ds(k * cap, cap), :] = jnp.zeros((cap, double), bf16)
    wcol[...] = jnp.broadcast_to(wrow_ref[...], (8, slots)).T[:, :1]
    pick[...] = (
        lax.broadcasted_iota(jnp.int32, (slots, span), 1) == wcol[...]
    ).astype(f32).astype(bf16)
    gain_row = gain_ref[...].reshape(1, width)
    for h, own in enumerate((tok_ref, gout_ref)):
        @pl.loop(0, width // COLS)
        def _(j):
            cols = pl.ds(pl.multiple_of(j * COLS, COLS), COLS)
            into = pl.ds(pl.multiple_of(h * width + j * COLS, COLS), COLS)
            xs[:, into] = nn(pick[:, :count], own[:, cols]).astype(bf16)
    for load in loads:
        load.wait()

    def fill(h):
        @pl.loop(0, width // COLS)
        def _(j):
            cols = pl.ds(pl.multiple_of(j * COLS, COLS), COLS)
            into = pl.ds(pl.multiple_of(h * width + j * COLS, COLS), COLS)
            come_in = nn(pick[:, count:], table[h, :, cols])
            xs[:, into] = (xs[:, into].astype(f32) + come_in).astype(bf16)

    wait_forward(0)
    fill(0)

    @pl.loop(0, windows)
    def _(w):
        rows = pl.ds(pl.multiple_of(w * WCAP, WCAP), WCAP)
        floats = xs[rows, :width].astype(f32)
        centred = floats - jnp.mean(floats, axis=-1, keepdims=True)
        inv_std = lax.rsqrt(jnp.mean(centred * centred, axis=-1, keepdims=True) + epsilon)
        u = centred * inv_std
        unit[rows, :] = u
        inv[rows, :] = inv_std
        normed[rows, :] = (u * gain_row).astype(bf16)

    normed_t[...] = normed[...].T

    @pl.loop(0, 3 * width // COLS)
    def _(j):
        cols = pl.ds(pl.multiple_of(j * COLS, COLS), COLS)
        packed[:, cols] = nn(normed[...], wqkv_ref[:, cols]).astype(bf16)

    wait_forward(1)
    fill(1)

    @pl.loop(0, width // COLS)
    def _(j):
        cols = pl.ds(pl.multiple_of(j * COLS, COLS), COLS)
        delta[:, cols] = nt(xs[:, width:], wout_ref[cols, :]).astype(bf16)

    def attention(group):
        @pl.loop(0, windows // 2)
        def _(turn):
            window(group, 2 * turn)
            window(group, 2 * turn + 1)

    def window(group, w):
        rows = pl.ds(pl.multiple_of(w * WCAP, WCAP), WCAP)
        valid = (wcol[rows, :] >= 0)[None]
        first = lax.broadcasted_iota(jnp.int32, (WCAP, pair), 1) < head_dim
        none = jnp.zeros((WCAP, pair), bf16)

        def split(t):
            return jnp.concatenate(
                [jnp.where(first, t, none), jnp.where(first, none, t)], axis=0
            )

        def join(t):
            return jnp.where(first, t[:WCAP], t[WCAP:])

        for j in (2 * group, 2 * group + 1):
            at = j * pair
            q = packed[rows, at:at + pair]
            k2 = split(packed[rows, width + at:width + at + pair])
            v2 = split(packed[rows, 2 * width + at:2 * width + at + pair])
            g = delta[rows, at:at + pair]
            scores = nt(k2, q).reshape(2, WCAP, WCAP) * scale
            scores = jnp.where(valid, scores, big_negative)
            top = jnp.max(scores, axis=1, keepdims=True)
            expo = jnp.exp(scores - top)
            probs = expo * (1.0 / jnp.sum(expo, axis=1, keepdims=True))
            weights = probs.reshape(2 * WCAP, WCAP).astype(bf16)
            mixed[rows, at:at + pair] = tn(weights, v2).astype(bf16)
            dweights = nt(v2, g).reshape(2, WCAP, WCAP)
            total = jnp.sum(dweights * probs, axis=1, keepdims=True)
            dscaled = (probs * (dweights - total) * scale).reshape(2 * WCAP, WCAP).astype(bf16)
            dpacked[rows, at:at + pair] = tn(dscaled, k2).astype(bf16)
            dpacked[rows, width + at:width + at + pair] = join(nn(dscaled, q)).astype(bf16)
            dpacked[rows, 2 * width + at:2 * width + at + pair] = join(
                nn(weights, g)
            ).astype(bf16)

    def first_column(p):
        return (p % 3) * width + (p // 3) * COLS if p < parts - 3 else 3 * width + (p - parts + 3) * COLS

    def gradient(at):
        if at < 3 * width:
            return nn(normed_t[...], dpacked[:, at:at + COLS])
        return nn(mixed_t[...], xs[:, at - 2 * width:at - 2 * width + COLS])

    def open_parts(members):
        for p in members:
            piece[p % 2] = gradient(first_column(p))
            rows = held[0].shape[2] // 2
            for c, position in enumerate(places[p]):
                both = piece[p % 2, c * rows:(c + 1) * rows, :]
                held[0][p, position] = jnp.concatenate(
                    [both[:, :HALF], both[:, HALF:]], axis=0
                ).astype(bf16)
            part_copy(p, 0).start()

    def advance(members, s):
        for p in members:
            part_copy(p, s).wait_recv()
            half = come[s].shape[1]
            base = own_bit(orders[p][s]) * half
            if s < stages - 1:
                step = min(half, 4)

                @pl.loop(0, half // step)
                def _(i):
                    mine = held[s][p, pl.ds(base + i * step, step)].astype(f32)
                    theirs = come[s][p, pl.ds(i * step, step)].astype(f32)
                    held[s + 1][p, pl.ds(i * step, step)] = (mine + theirs).astype(bf16)

                part_copy(p, s + 1).start()
            else:
                mine = held[s][p, pl.ds(base, 1)].astype(f32)
                total = mine[0] + come[s][p, 0].astype(f32)
                rows = total.shape[0] // 2
                for i in range(2):
                    at = first_column(p) + i * HALF
                    value = total[i * rows:(i + 1) * rows]
                    if at < 3 * width:
                        gqkv_ref[:, at:at + HALF] = value
                    else:
                        gproj_ref[:, at - 3 * width:at - 3 * width + HALF] = value

    def advance_gain(s):
        gain_copy(s).wait_recv()
        total = gheld[s] + gcome[s]
        if s < stages - 1:
            gheld[s + 1] = total
            gain_copy(s + 1).start()
        else:
            gsum_ref[...] = total

    groups = HEADS // 4
    waves = [range(3 * i, 3 * i + 3) for i in range(parts // 3)]
    stage_of = {}

    def open_wave(i):
        if parts:
            open_parts(waves[i])
            turn()
            stage_of[i] = 0

    def turn():
        for i in sorted(stage_of):
            if stage_of[i] < stages:
                advance(waves[i], stage_of[i])
                stage_of[i] += 1

    for group in range(groups):
        attention(group)
        open_wave(group)

    mixed_t[...] = mixed[...].T
    open_wave(groups)

    @pl.loop(0, width // COLS)
    def _(j):
        cols = pl.ds(pl.multiple_of(j * COLS, COLS), COLS)
        out = nn(mixed[...], wout_ref[:, cols])
        bg[:, cols] = (xs[:, cols].astype(f32) + out).astype(bf16)
        dnormed[:, cols] = nt(dpacked[...], wqkv_ref[cols, :]).astype(bf16)

    turn()
    gheld[0] = jnp.zeros((8, width), f32)

    @pl.loop(0, windows)
    def _(w):
        rows = pl.ds(pl.multiple_of(w * WCAP, WCAP), WCAP)
        dn = dnormed[rows, :].astype(f32)
        u = unit[rows, :]
        gheld[0] += jnp.sum((dn * u).reshape(WCAP // 8, 8, width), axis=0)
        dunit = dn * gain_row
        dcentre = inv[rows, :] * (
            dunit
            - jnp.mean(dunit, axis=-1, keepdims=True)
            - u * jnp.mean(dunit * u, axis=-1, keepdims=True)
        )
        bg[rows, width:] = (xs[rows, width:].astype(f32) + dcentre).astype(bf16)

    gain_copy(0).start()
    received = (
        lax.broadcasted_iota(jnp.int32, (7 * cap, slots), 0) + count == wrow_ref[...]
    ).astype(f32).astype(bf16)
    for j in range(double // COLS):
        cols = slice(j * COLS, (j + 1) * COLS)
        ret[:, cols] = nn(received, bg[:, cols]).astype(bf16)
    for k in (6, 5, 4, 3, 2, 1, 0):
        @pl.when(found[k][3])
        def _():
            return_copy(k).start()
    turn()
    kept = (
        lax.broadcasted_iota(jnp.int32, (count, slots), 0) == wrow_ref[...]
    ).astype(f32).astype(bf16)
    for j in range(double // COLS):
        cols = slice(j * COLS, (j + 1) * COLS)
        own_ref[:, cols] = nn(kept, bg[:, cols]).astype(bf16)

    if not parts:
        for j in range(4 * width // COLS):
            grad_ref[:, j * COLS:(j + 1) * COLS] = gradient(j * COLS)
    for s in range(stages):
        turn()
        advance_gain(s)

    for k in range(7):
        @pl.when(found[k][2])
        def _():
            return_copy(k).wait_recv()

        @pl.when(found[k][3])
        def _():
            return_copy(k).wait_send()
    for s in range(stages):
        for p in range(parts):
            part_copy(p, s).wait_send()
        gain_copy(s).wait_send()


def finish_kernel(sizes, own_ref, back_ref, place_ref, gsum_ref, *refs):
    many = len(refs) // 2 - 1
    given, (block_ref, gtok_ref, gain_ref, *final) = refs[:many], refs[many:]
    width = block_ref.shape[1]
    chunk = gain_ref.shape[1]
    place = place_ref[...]
    block_ref[...] = (
        own_ref[:, :width].astype(f32) + nn(place, back_ref[:, :width])
    ).astype(bf16)
    gtok_ref[...] = (
        own_ref[:, width:].astype(f32) + nn(place, back_ref[:, width:])
    ).astype(bf16)
    me = (lax.axis_index("gx") * sizes[1] + lax.axis_index("gy")) * sizes[2] + lax.axis_index("gz")
    rolled = pltpu.roll(gsum_ref[...], lax.rem(width - me * chunk, width), 1)
    gain_ref[...] = jnp.sum(rolled, axis=0, keepdims=True)[:, :chunk]
    for source, target in zip(given, final):
        target[...] = source[...]


def on_device(sizes, tokens, norm_gain, w_qkv, w_out, send_rows, window_rows, grad_out):
    count, width = tokens.shape
    slots = window_rows.shape[1]
    cap = send_rows.shape[2]
    span = count + 7 * cap
    devices = sizes[0] * sizes[1] * sizes[2]
    vmem = pl.BlockSpec(memory_space=pltpu.VMEM)
    params = functools.partial(pltpu.CompilerParams, vmem_limit_bytes=VMEM_BYTES)

    by_axis = [[(a, 1 << i) for i in range(sizes[a].bit_length() - 1)] for a in range(3)]
    x_bits, y_bits, z_bits = by_axis
    bits = y_bits + x_bits + z_bits
    chunk = width // devices
    grouped = (
        all(1 << len(b) == n for b, n in zip(by_axis, sizes))
        and len(y_bits) > 0
        and chunk * devices == width
        and chunk % 8 == 0
    )
    parts = 4 * width // COLS
    orders, places = [], None
    if grouped:
        rest = y_bits[1:]
        kinds = [
            y_bits[:1] + x_bits + rest + z_bits,
            y_bits[:1] + rest + x_bits + z_bits,
            y_bits[:1] + z_bits + x_bits + rest,
        ]
        orders = [kinds[PLAN[p % len(PLAN)]] for p in range(parts)]

        def position(order, c):
            at = (c // (sizes[1] * sizes[2]), c // sizes[2] % sizes[1], c % sizes[2])
            value = 0
            for axis, distance in order:
                value = 2 * value + at[axis] // distance % 2
            return value

        places = [[position(order, c) for c in range(devices)] for order in orders]

    stages = len(bits)
    anywhere = pl.BlockSpec(memory_space=pl.ANY)
    out_shape = [
        jax.ShapeDtypeStruct((count, 2 * width), bf16),
        jax.ShapeDtypeStruct((7 * cap, 2 * width), bf16),
        jax.ShapeDtypeStruct((count, 7 * cap), bf16),
        jax.ShapeDtypeStruct((8, width), f32),
    ]
    if grouped:
        sums = [
            jax.ShapeDtypeStruct((chunk, 3 * width), f32),
            jax.ShapeDtypeStruct((chunk, width), f32),
        ]
    else:
        sums = [jax.ShapeDtypeStruct((width, 4 * width), f32)]
    scratch = [
        pltpu.VMEM((2, 7 * cap, width), bf16),
        pltpu.VMEM((2, 7 * cap, width), bf16),
        pltpu.VMEM((width, 3 * width), bf16),
        pltpu.VMEM((width, width), bf16),
        pltpu.VMEM((slots, 1), jnp.int32),
        pltpu.VMEM((slots, span), bf16),
        pltpu.VMEM((slots, 2 * width), bf16),
        pltpu.VMEM((slots, width), f32),
        pltpu.VMEM((slots, width), bf16),
        pltpu.VMEM((width, slots), bf16),
        pltpu.VMEM((slots, 1), f32),
        pltpu.VMEM((slots, 3 * width), bf16),
        pltpu.VMEM((slots, width), bf16),
        pltpu.VMEM((slots, width), bf16),
        pltpu.VMEM((width, slots), bf16),
        pltpu.VMEM((slots, 3 * width), bf16),
        pltpu.VMEM((slots, width), bf16),
        pltpu.VMEM((slots, 2 * width), bf16),
        pltpu.VMEM((7 * cap, 2 * width), bf16),
        pltpu.VMEM((stages, 8, width), f32),
        pltpu.VMEM((stages, 8, width), f32),
        pltpu.SemaphoreType.DMA((2,)),
        pltpu.SemaphoreType.DMA((14,)),
        pltpu.SemaphoreType.DMA((14,)),
        pltpu.SemaphoreType.DMA((7,)),
        pltpu.SemaphoreType.DMA((7,)),
        pltpu.SemaphoreType.DMA((stages,)),
        pltpu.SemaphoreType.DMA((stages,)),
    ]
    if grouped:
        slab = (2 * chunk, HALF)
        scratch += [pltpu.VMEM((2, width, COLS), f32)]
        scratch += [pltpu.SemaphoreType.DMA((parts * stages,))] * 2
        scratch += [pltpu.VMEM((parts, devices >> (s + 1)) + slab, bf16) for s in range(stages)]
        scratch += [pltpu.VMEM((parts, devices >> s) + slab, bf16) for s in range(stages)]
    own, back, place, gain_sum, *grads = pl.pallas_call(
        functools.partial(block_kernel, sizes, orders, bits, places),
        out_shape=tuple(out_shape + sums),
        in_specs=[vmem] * 5 + [anywhere] * 2,
        out_specs=(vmem,) * len(out_shape + sums),
        scratch_shapes=scratch,
        compiler_params=params(collective_id=0, has_side_effects=True),
        name="block",
    )(tokens, grad_out, jnp.transpose(send_rows, (1, 0, 2)), window_rows, norm_gain, w_qkv, w_out)

    passed = grads if grouped else []
    final_shape = [jax.ShapeDtypeStruct((count, width), bf16)] * 2
    final_shape += [jax.ShapeDtypeStruct((1, chunk), f32)] + (sums if grouped else [])
    block_out, grad_tokens, grad_gain, *final = pl.pallas_call(
        functools.partial(finish_kernel, sizes),
        out_shape=tuple(final_shape),
        in_specs=[vmem] * (4 + len(passed)),
        out_specs=(vmem,) * len(final_shape),
        compiler_params=params(),
        name="finish",
    )(own, back, place, gain_sum, *passed)
    if grouped:
        grad_qkv, grad_proj = final
    else:
        summed = lax.psum_scatter(grads[0], AXES, scatter_dimension=0, tiled=True)
        grad_qkv, grad_proj = summed[:, :3 * width], summed[:, 3 * width:]
    return (block_out, grad_tokens, grad_gain.reshape(chunk), grad_qkv, grad_proj)


def solution(mesh):
    sizes = tuple(mesh.shape[a] for a in AXES)
    in_specs = (
        P(AXES, None),
        P(),
        P(),
        P(),
        P(AXES, None, None),
        P(AXES, None),
        P(AXES, None),
    )
    out_specs = (
        P(AXES, None),
        P(AXES, None),
        P(AXES),
        P(AXES, None),
        P(AXES, None),
    )
    return jax.shard_map(
        functools.partial(on_device, sizes),
        mesh=mesh,
        in_specs=in_specs,
        out_specs=out_specs,
        check_vma=False,
    )
```

```python
import functools

import jax
import jax.numpy as jnp
from jax import lax
from jax.experimental import pallas as pl
from jax.experimental.pallas import tpu as pltpu
from jax.sharding import PartitionSpec as P

HEADS = 12
WCAP = 128
COLS = 256
HALF = 128
VMEM_BYTES = 56 * 1024 * 1024

epsilon = 1e-06
big_negative = -1e30

AXES = ("gx", "gy", "gz")
MESH = pl.DeviceIdType.MESH
f32 = jnp.float32
bf16 = jnp.bfloat16


def nn(a, b):
    return lax.dot_general(a, b, (((1,), (0,)), ((), ())), preferred_element_type=f32)


def nt(a, b):
    return lax.dot_general(a, b, (((1,), (1,)), ((), ())), preferred_element_type=f32)


def tn(a, b):
    return lax.dot_general(a, b, (((0,), (0,)), ((), ())), preferred_element_type=f32)


def direction(k):
    return (k // 4, k // 2 % 2, k % 2)


def neighbours(sizes):
    here = [lax.axis_index(a) for a in AXES]
    found = []
    for k in range(1, 8):
        step = direction(k)
        up = tuple(here[i] + step[i] for i in range(3))
        down = tuple(here[i] - step[i] for i in range(3))
        has_up = functools.reduce(
            jnp.logical_and, [up[i] < sizes[i] for i in range(3) if step[i]]
        )
        has_down = functools.reduce(
            jnp.logical_and, [down[i] >= 0 for i in range(3) if step[i]]
        )
        found.append((up, down, has_up, has_down))
    return found


def greet(found, partners):
    barrier = pltpu.get_barrier_semaphore()
    count = jnp.int32(len(partners))
    for up, down, has_up, has_down in found:
        @pl.when(has_up)
        def _():
            pl.semaphore_signal(barrier, inc=1, device_id=up, device_id_type=MESH)

        @pl.when(has_down)
        def _():
            pl.semaphore_signal(barrier, inc=1, device_id=down, device_id_type=MESH)

        count = count + has_up.astype(jnp.int32) + has_down.astype(jnp.int32)
    for partner in partners:
        pl.semaphore_signal(barrier, inc=1, device_id=partner, device_id_type=MESH)
    pl.semaphore_wait(barrier, count)


def block_kernel(sizes, orders, bits, places, *refs):
    parts, pairs = len(orders), len(bits)
    stages = pairs + 1
    deep = sizes[2]
    refs = list(refs)

    def take(n):
        out = refs[:n]
        del refs[:n]
        return out

    tok_ref, gout_ref, send_ref, wrow_ref, gain_ref, wqkv_hbm, wout_hbm = take(7)
    own_ref, back_ref, place_ref, gsum_ref = take(4)
    if parts:
        gqkv_ref, gproj_ref = take(2)
    else:
        (grad_ref,) = take(1)
    buf, table, wqkv_ref, wout_ref, wcol, pick = take(6)
    xs, unit, normed, normed_t, inv, packed, delta, mixed, mixed_t, dpacked, dnormed = take(11)
    bg, ret, held_probs = take(3)
    gheld, gcome, gcome_z = take(3)
    load_sem, send_sem, recv_sem, ret_send, ret_recv, gain_send, gain_recv = take(7)
    gain_send_z, gain_recv_z = take(2)
    if parts:
        piece, part_send, part_recv, send_z, recv_z, come_z = take(6)
        come = take(pairs)
        held = take(stages)

    found = neighbours(sizes)
    count, width = tok_ref.shape
    double = 2 * width
    cap = send_ref.shape[2]
    span = count + 7 * cap
    slots = wrow_ref.shape[1]
    windows = slots // WCAP
    head_dim = width // HEADS
    pair = 2 * head_dim
    scale = head_dim ** (-0.5)
    here = [lax.axis_index(a) for a in AXES]

    def own_bit(bit):
        axis, distance = bit
        return here[axis] // distance % 2

    def partner(bit):
        axis, distance = bit
        return tuple(
            here[i] + distance * (1 - 2 * own_bit(bit)) if i == axis else here[i] for i in range(3)
        )

    def forward_copy(h, k):
        return pltpu.make_async_remote_copy(
            src_ref=buf.at[h, pl.ds(k * cap, cap)],
            dst_ref=table.at[h, pl.ds(k * cap, cap)],
            send_sem=send_sem.at[7 * h + k],
            recv_sem=recv_sem.at[7 * h + k],
            device_id=found[k][0],
            device_id_type=MESH,
        )

    def along_z(d):
        return (here[0], here[1], lax.rem(here[2] + d, deep))

    def return_copy(h, k):
        return pltpu.make_async_remote_copy(
            src_ref=ret.at[h, pl.ds(k * cap, cap)],
            dst_ref=back_ref.at[h, pl.ds(k * cap, cap)],
            send_sem=ret_send.at[7 * h + k],
            recv_sem=ret_recv.at[7 * h + k],
            device_id=found[k][1],
            device_id_type=MESH,
        )

    def part_copy_z(p, d):
        return pltpu.make_async_remote_copy(
            src_ref=held[pairs].at[p, pl.ds(along_z(d)[2], 1)],
            dst_ref=come_z.at[p, pl.ds(d - 1, 1)],
            send_sem=send_z.at[p * (deep - 1) + d - 1],
            recv_sem=recv_z.at[p * (deep - 1) + d - 1],
            device_id=along_z(d),
            device_id_type=MESH,
        )

    def gain_copy_z(d):
        return pltpu.make_async_remote_copy(
            src_ref=gheld.at[pairs],
            dst_ref=gcome_z.at[d - 1],
            send_sem=gain_send_z.at[d - 1],
            recv_sem=gain_recv_z.at[d - 1],
            device_id=along_z(d),
            device_id_type=MESH,
        )

    def part_copy(p, s):
        bit = orders[p][s]
        half = come[s].shape[1]
        return pltpu.make_async_remote_copy(
            src_ref=held[s].at[p, pl.ds((1 - own_bit(bit)) * half, half)],
            dst_ref=come[s].at[p],
            send_sem=part_send.at[p * pairs + s],
            recv_sem=part_recv.at[p * pairs + s],
            device_id=partner(bit),
            device_id_type=MESH,
        )

    def gain_copy(s):
        return pltpu.make_async_remote_copy(
            src_ref=gheld.at[s],
            dst_ref=gcome.at[s],
            send_sem=gain_send.at[s],
            recv_sem=gain_recv.at[s],
            device_id=partner(bits[s]),
            device_id_type=MESH,
        )

    loads = [
        pltpu.make_async_copy(wqkv_hbm, wqkv_ref, load_sem.at[0]),
        pltpu.make_async_copy(wout_hbm, wout_ref, load_sem.at[1]),
    ]
    for load in loads:
        load.start()

    send_row = jnp.concatenate([send_ref[k] for k in range(7)], axis=1)
    place = (
        lax.broadcasted_iota(jnp.int32, (count, 7 * cap), 0) == send_row
    ).astype(f32).astype(bf16)
    place_ref[...] = place
    buf[0] = tn(place, tok_ref[...]).astype(bf16)
    greet(found, [partner(bit) for bit in bits] + [along_z(d) for d in range(1, deep)])

    def start_forward(h):
        for k in (6, 5, 4, 3, 2, 1, 0):
            @pl.when(found[k][2])
            def _():
                forward_copy(h, k).start()

    def wait_forward(h):
        for k in range(7):
            @pl.when(found[k][3])
            def _():
                forward_copy(h, k).wait_recv()

    start_forward(0)
    buf[1] = tn(place, gout_ref[...]).astype(bf16)
    start_forward(1)
    for k in range(7):
        @pl.when(jnp.logical_not(found[k][3]))
        def _():
            for h in range(2):
                table[h, pl.ds(k * cap, cap), :] = jnp.zeros((cap, width), bf16)

        @pl.when(jnp.logical_not(found[k][2]))
        def _():
            for h in range(2):
                back_ref[h, pl.ds(k * cap, cap), :] = jnp.zeros((cap, width), bf16)
    wcol[...] = jnp.broadcast_to(wrow_ref[...], (8, slots)).T[:, :1]
    pick[...] = (
        lax.broadcasted_iota(jnp.int32, (slots, span), 1) == wcol[...]
    ).astype(f32).astype(bf16)
    gain_row = gain_ref[...].reshape(1, width)
    for h, own in enumerate((tok_ref, gout_ref)):
        @pl.loop(0, width // COLS)
        def _(j):
            cols = pl.ds(pl.multiple_of(j * COLS, COLS), COLS)
            into = pl.ds(pl.multiple_of(h * width + j * COLS, COLS), COLS)
            xs[:, into] = nn(pick[:, :count], own[:, cols]).astype(bf16)
    for load in loads:
        load.wait()

    def fill(h):
        @pl.loop(0, width // COLS)
        def _(j):
            cols = pl.ds(pl.multiple_of(j * COLS, COLS), COLS)
            into = pl.ds(pl.multiple_of(h * width + j * COLS, COLS), COLS)
            come_in = nn(pick[:, count:], table[h, :, cols])
            xs[:, into] = (xs[:, into].astype(f32) + come_in).astype(bf16)

    wait_forward(0)
    fill(0)

    @pl.loop(0, windows)
    def _(w):
        rows = pl.ds(pl.multiple_of(w * WCAP, WCAP), WCAP)
        floats = xs[rows, :width].astype(f32)
        centred = floats - jnp.mean(floats, axis=-1, keepdims=True)
        inv_std = lax.rsqrt(jnp.mean(centred * centred, axis=-1, keepdims=True) + epsilon)
        u = centred * inv_std
        unit[rows, :] = u
        inv[rows, :] = inv_std
        normed[rows, :] = (u * gain_row).astype(bf16)

    normed_t[...] = normed[...].T

    @pl.loop(0, 3 * width // COLS)
    def _(j):
        cols = pl.ds(pl.multiple_of(j * COLS, COLS), COLS)
        packed[:, cols] = nn(normed[...], wqkv_ref[:, cols]).astype(bf16)

    first = lax.broadcasted_iota(jnp.int32, (WCAP, pair), 1) < head_dim
    none = jnp.zeros((WCAP, pair), bf16)

    def split(t):
        return jnp.concatenate([jnp.where(first, t, none), jnp.where(first, none, t)], axis=0)

    def join(t):
        return jnp.where(first, t[:WCAP], t[WCAP:])

    def both_heads(w):
        return pl.ds(pl.multiple_of(w * 2 * WCAP, 2 * WCAP), 2 * WCAP)

    def forward(w, j, valid):
        rows = pl.ds(pl.multiple_of(w * WCAP, WCAP), WCAP)
        at = j * pair
        q = packed[rows, at:at + pair]
        k2 = split(packed[rows, width + at:width + at + pair])
        v2 = split(packed[rows, 2 * width + at:2 * width + at + pair])
        scores = nt(k2, q).reshape(2, WCAP, WCAP) * scale
        scores = jnp.where(valid, scores, big_negative)
        top = jnp.max(scores, axis=1, keepdims=True)
        expo = jnp.exp(scores - top)
        probs = expo * (1.0 / jnp.sum(expo, axis=1, keepdims=True))
        probs = probs.reshape(2 * WCAP, WCAP)
        held_probs[j, both_heads(w), :] = probs
        mixed[rows, at:at + pair] = tn(probs.astype(bf16), v2).astype(bf16)

    def backward(w, j):
        rows = pl.ds(pl.multiple_of(w * WCAP, WCAP), WCAP)
        at = j * pair
        q = packed[rows, at:at + pair]
        k2 = split(packed[rows, width + at:width + at + pair])
        v2 = split(packed[rows, 2 * width + at:2 * width + at + pair])
        g = delta[rows, at:at + pair]
        probs = held_probs[j, both_heads(w), :]
        weights = probs.astype(bf16)
        probs = probs.reshape(2, WCAP, WCAP)
        dweights = nt(v2, g).reshape(2, WCAP, WCAP)
        total = jnp.sum(dweights * probs, axis=1, keepdims=True)
        dscaled = (probs * (dweights - total) * scale).reshape(2 * WCAP, WCAP).astype(bf16)
        dpacked[rows, at:at + pair] = tn(dscaled, k2).astype(bf16)
        dpacked[rows, width + at:width + at + pair] = join(nn(dscaled, q)).astype(bf16)
        dpacked[rows, 2 * width + at:2 * width + at + pair] = join(nn(weights, g)).astype(bf16)

    def backward_group(group):
        @pl.loop(0, windows // 2)
        def _(i):
            for w in (2 * i, 2 * i + 1):
                for j in (2 * group, 2 * group + 1):
                    backward(w, j)

    @pl.loop(0, windows)
    def _(w):
        valid = (wcol[pl.ds(pl.multiple_of(w * WCAP, WCAP), WCAP), :] >= 0)[None]
        for j in range(HEADS // 2):
            forward(w, j, valid)

    @pl.loop(0, width // COLS)
    def _(j):
        cols = pl.ds(pl.multiple_of(j * COLS, COLS), COLS)
        out = nn(mixed[...], wout_ref[:, cols])
        bg[:, cols] = (xs[:, cols].astype(f32) + out).astype(bf16)

    received = (
        lax.broadcasted_iota(jnp.int32, (7 * cap, slots), 0) + count == wrow_ref[...]
    ).astype(f32).astype(bf16)

    def collect_returns(h):
        for j in range(width // COLS):
            cols = slice(j * COLS, (j + 1) * COLS)
            into = slice(h * width + j * COLS, h * width + (j + 1) * COLS)
            ret[h, :, cols] = nn(received, bg[:, into]).astype(bf16)

    def start_returns(h, members):
        for k in members:
            @pl.when(found[k][3])
            def _():
                return_copy(h, k).start()

    collect_returns(0)
    start_returns(0, (6, 5, 4, 3, 2, 1, 0))

    wait_forward(1)
    fill(1)

    @pl.loop(0, width // COLS)
    def _(j):
        cols = pl.ds(pl.multiple_of(j * COLS, COLS), COLS)
        delta[:, cols] = nt(xs[:, width:], wout_ref[cols, :]).astype(bf16)

    def first_column(p):
        if p < 3:
            return 3 * width + p * COLS
        return (p % 3) * width + (p // 3 - 1) * COLS

    def gradient(at):
        if at < 3 * width:
            return nn(normed_t[...], dpacked[:, at:at + COLS])
        return nn(mixed_t[...], xs[:, at - 2 * width:at - 2 * width + COLS])

    def open_parts(members):
        for p in members:
            piece[p % 2] = gradient(first_column(p))
            rows = held[0].shape[2] // 2
            for c, position in enumerate(places[p]):
                both = piece[p % 2, c * rows:(c + 1) * rows, :]
                held[0][p, position] = jnp.concatenate(
                    [both[:, :HALF], both[:, HALF:]], axis=0
                ).astype(bf16)
            part_copy(p, 0).start()

    def advance(members, s):
        for p in members:
            if s < pairs:
                part_copy(p, s).wait_recv()
                half = come[s].shape[1]
                base = own_bit(orders[p][s]) * half
                step = min(half, 4)

                @pl.loop(0, half // step)
                def _(i):
                    mine = held[s][p, pl.ds(base + i * step, step)].astype(f32)
                    theirs = come[s][p, pl.ds(i * step, step)].astype(f32)
                    held[s + 1][p, pl.ds(i * step, step)] = (mine + theirs).astype(bf16)

                if s + 1 < pairs:
                    part_copy(p, s + 1).start()
                else:
                    for d in range(1, deep):
                        part_copy_z(p, d).start()
            else:
                total = held[s][p, pl.ds(here[2], 1)].astype(f32)[0]
                for d in range(1, deep):
                    part_copy_z(p, d).wait_recv()
                    total = total + come_z[p, d - 1].astype(f32)
                rows = total.shape[0] // 2
                for i in range(2):
                    at = first_column(p) + i * HALF
                    value = total[i * rows:(i + 1) * rows]
                    if at < 3 * width:
                        gqkv_ref[:, at:at + HALF] = value
                    else:
                        gproj_ref[:, at - 3 * width:at - 3 * width + HALF] = value

    def advance_gain(s):
        if s < pairs:
            gain_copy(s).wait_recv()
            gheld[s + 1] = gheld[s] + gcome[s]
            if s + 1 < pairs:
                gain_copy(s + 1).start()
            else:
                for d in range(1, deep):
                    gain_copy_z(d).start()
        else:
            total = gheld[s]
            for d in range(1, deep):
                gain_copy_z(d).wait_recv()
                total = total + gcome_z[d - 1]
            gsum_ref[...] = total

    groups = HEADS // 4
    waves = [range(3 * i, 3 * i + 3) for i in range(parts // 3)]
    stage_of = {}

    def open_wave(i):
        if parts:
            open_parts(waves[i])
            turn()
            stage_of[i] = 0

    def turn():
        for i in sorted(stage_of):
            if stage_of[i] < stages:
                advance(waves[i], stage_of[i])
                stage_of[i] += 1

    mixed_t[...] = mixed[...].T
    open_wave(0)
    for group in range(groups):
        backward_group(group)
        open_wave(group + 1)

    @pl.loop(0, width // COLS)
    def _(j):
        cols = pl.ds(pl.multiple_of(j * COLS, COLS), COLS)
        dnormed[:, cols] = nt(dpacked[...], wqkv_ref[cols, :]).astype(bf16)

    turn()
    gheld[0] = jnp.zeros((8, width), f32)

    @pl.loop(0, windows)
    def _(w):
        rows = pl.ds(pl.multiple_of(w * WCAP, WCAP), WCAP)
        dn = dnormed[rows, :].astype(f32)
        u = unit[rows, :]
        gheld[0] += jnp.sum((dn * u).reshape(WCAP // 8, 8, width), axis=0)
        dunit = dn * gain_row
        dcentre = inv[rows, :] * (
            dunit
            - jnp.mean(dunit, axis=-1, keepdims=True)
            - u * jnp.mean(dunit * u, axis=-1, keepdims=True)
        )
        bg[rows, width:] = (xs[rows, width:].astype(f32) + dcentre).astype(bf16)

    gain_copy(0).start()
    collect_returns(1)
    start_returns(1, (6, 5, 4, 3))
    turn()
    advance_gain(0)
    start_returns(1, (2, 1, 0))
    kept = (
        lax.broadcasted_iota(jnp.int32, (count, slots), 0) == wrow_ref[...]
    ).astype(f32).astype(bf16)
    for j in range(double // COLS):
        cols = slice(j * COLS, (j + 1) * COLS)
        own_ref[:, cols] = nn(kept, bg[:, cols]).astype(bf16)

    if not parts:
        for j in range(4 * width // COLS):
            grad_ref[:, j * COLS:(j + 1) * COLS] = gradient(j * COLS)
    for s in range(1, stages):
        turn()
        advance_gain(s)

    for h in range(2):
        for k in range(7):
            @pl.when(found[k][2])
            def _():
                return_copy(h, k).wait_recv()
                forward_copy(h, k).wait_send()

            @pl.when(found[k][3])
            def _():
                return_copy(h, k).wait_send()
    for s in range(pairs):
        for p in range(parts):
            part_copy(p, s).wait_send()
        gain_copy(s).wait_send()
    for d in range(1, deep):
        for p in range(parts):
            part_copy_z(p, d).wait_send()
        gain_copy_z(d).wait_send()


def finish_kernel(sizes, own_ref, back_ref, place_ref, gsum_ref, *refs):
    many = len(refs) // 2 - 1
    given, (block_ref, gtok_ref, gain_ref, *final) = refs[:many], refs[many:]
    width = block_ref.shape[1]
    chunk = gain_ref.shape[1]
    place = place_ref[...]
    block_ref[...] = (
        own_ref[:, :width].astype(f32) + nn(place, back_ref[0])
    ).astype(bf16)
    gtok_ref[...] = (
        own_ref[:, width:].astype(f32) + nn(place, back_ref[1])
    ).astype(bf16)
    me = (lax.axis_index("gx") * sizes[1] + lax.axis_index("gy")) * sizes[2] + lax.axis_index("gz")
    rolled = pltpu.roll(gsum_ref[...], lax.rem(width - me * chunk, width), 1)
    gain_ref[...] = jnp.sum(rolled, axis=0, keepdims=True)[:, :chunk]
    for source, target in zip(given, final):
        target[...] = source[...]


def on_device(sizes, tokens, norm_gain, w_qkv, w_out, send_rows, window_rows, grad_out):
    count, width = tokens.shape
    slots = window_rows.shape[1]
    cap = send_rows.shape[2]
    span = count + 7 * cap
    devices = sizes[0] * sizes[1] * sizes[2]
    vmem = pl.BlockSpec(memory_space=pltpu.VMEM)
    params = functools.partial(pltpu.CompilerParams, vmem_limit_bytes=VMEM_BYTES)

    by_axis = [[(a, 1 << i) for i in range(sizes[a].bit_length() - 1)] for a in range(3)]
    x_bits, y_bits, z_bits = by_axis
    bits = y_bits + x_bits
    chunk = width // devices
    grouped = (
        all(1 << len(b) == n for b, n in zip(by_axis, sizes))
        and len(y_bits) > 0
        and sizes[2] > 1
        and chunk * devices == width
        and chunk % 8 == 0
    )
    parts = 4 * width // COLS
    orders, places = [], None
    if grouped:
        rest = y_bits[1:]
        kinds = [y_bits[:1] + x_bits + rest, y_bits[:1] + rest + x_bits]
        orders = [kinds[p % 2] for p in range(parts)]

        def position(order, c):
            at = (c // (sizes[1] * sizes[2]), c // sizes[2] % sizes[1], c % sizes[2])
            value = 0
            for axis, distance in order:
                value = 2 * value + at[axis] // distance % 2
            return value * sizes[2] + at[2]

        places = [[position(order, c) for c in range(devices)] for order in orders]

    pairs, deep = len(bits), sizes[2]
    anywhere = pl.BlockSpec(memory_space=pl.ANY)
    out_shape = [
        jax.ShapeDtypeStruct((count, 2 * width), bf16),
        jax.ShapeDtypeStruct((2, 7 * cap, width), bf16),
        jax.ShapeDtypeStruct((count, 7 * cap), bf16),
        jax.ShapeDtypeStruct((8, width), f32),
    ]
    if grouped:
        sums = [
            jax.ShapeDtypeStruct((chunk, 3 * width), f32),
            jax.ShapeDtypeStruct((chunk, width), f32),
        ]
    else:
        sums = [jax.ShapeDtypeStruct((width, 4 * width), f32)]
    scratch = [
        pltpu.VMEM((2, 7 * cap, width), bf16),
        pltpu.VMEM((2, 7 * cap, width), bf16),
        pltpu.VMEM((width, 3 * width), bf16),
        pltpu.VMEM((width, width), bf16),
        pltpu.VMEM((slots, 1), jnp.int32),
        pltpu.VMEM((slots, span), bf16),
        pltpu.VMEM((slots, 2 * width), bf16),
        pltpu.VMEM((slots, width), f32),
        pltpu.VMEM((slots, width), bf16),
        pltpu.VMEM((width, slots), bf16),
        pltpu.VMEM((slots, 1), f32),
        pltpu.VMEM((slots, 3 * width), bf16),
        pltpu.VMEM((slots, width), bf16),
        pltpu.VMEM((slots, width), bf16),
        pltpu.VMEM((width, slots), bf16),
        pltpu.VMEM((slots, 3 * width), bf16),
        pltpu.VMEM((slots, width), bf16),
        pltpu.VMEM((slots, 2 * width), bf16),
        pltpu.VMEM((2, 7 * cap, width), bf16),
        pltpu.VMEM((HEADS // 2, 2 * slots, WCAP), f32),
        pltpu.VMEM((pairs + 1, 8, width), f32),
        pltpu.VMEM((pairs, 8, width), f32),
        pltpu.VMEM((deep - 1, 8, width), f32),
        pltpu.SemaphoreType.DMA((2,)),
        pltpu.SemaphoreType.DMA((14,)),
        pltpu.SemaphoreType.DMA((14,)),
        pltpu.SemaphoreType.DMA((14,)),
        pltpu.SemaphoreType.DMA((14,)),
        pltpu.SemaphoreType.DMA((pairs,)),
        pltpu.SemaphoreType.DMA((pairs,)),
        pltpu.SemaphoreType.DMA((deep - 1,)),
        pltpu.SemaphoreType.DMA((deep - 1,)),
    ]
    if grouped:
        slab = (2 * chunk, HALF)
        scratch += [pltpu.VMEM((2, width, COLS), f32)]
        scratch += [pltpu.SemaphoreType.DMA((parts * pairs,))] * 2
        scratch += [pltpu.SemaphoreType.DMA((parts * (deep - 1),))] * 2
        scratch += [pltpu.VMEM((parts, deep - 1) + slab, bf16)]
        scratch += [pltpu.VMEM((parts, devices >> (s + 1)) + slab, bf16) for s in range(pairs)]
        scratch += [pltpu.VMEM((parts, devices >> s) + slab, bf16) for s in range(pairs + 1)]
    own, back, place, gain_sum, *grads = pl.pallas_call(
        functools.partial(block_kernel, sizes, orders, bits, places),
        out_shape=tuple(out_shape + sums),
        in_specs=[vmem] * 5 + [anywhere] * 2,
        out_specs=(vmem,) * len(out_shape + sums),
        scratch_shapes=scratch,
        compiler_params=params(collective_id=0, has_side_effects=True),
        name="block",
    )(tokens, grad_out, jnp.transpose(send_rows, (1, 0, 2)), window_rows, norm_gain, w_qkv, w_out)

    passed = grads if grouped else []
    final_shape = [jax.ShapeDtypeStruct((count, width), bf16)] * 2
    final_shape += [jax.ShapeDtypeStruct((1, chunk), f32)] + (sums if grouped else [])
    block_out, grad_tokens, grad_gain, *final = pl.pallas_call(
        functools.partial(finish_kernel, sizes),
        out_shape=tuple(final_shape),
        in_specs=[vmem] * (4 + len(passed)),
        out_specs=(vmem,) * len(final_shape),
        compiler_params=params(),
        name="finish",
    )(own, back, place, gain_sum, *passed)
    if grouped:
        grad_qkv, grad_proj = final
    else:
        summed = lax.psum_scatter(grads[0], AXES, scatter_dimension=0, tiled=True)
        grad_qkv, grad_proj = summed[:, :3 * width], summed[:, 3 * width:]
    return (block_out, grad_tokens, grad_gain.reshape(chunk), grad_qkv, grad_proj)


def solution(mesh):
    sizes = tuple(mesh.shape[a] for a in AXES)
    in_specs = (
        P(AXES, None),
        P(),
        P(),
        P(),
        P(AXES, None, None),
        P(AXES, None),
        P(AXES, None),
    )
    out_specs = (
        P(AXES, None),
        P(AXES, None),
        P(AXES),
        P(AXES, None),
        P(AXES, None),
    )
    return jax.shard_map(
        functools.partial(on_device, sizes),
        mesh=mesh,
        in_specs=in_specs,
        out_specs=out_specs,
        check_vma=False,
    )
```

```python
import functools

import jax
import jax.numpy as jnp
from jax import lax
from jax.experimental import pallas as pl
from jax.experimental.pallas import tpu as pltpu
from jax.sharding import PartitionSpec as P

HEADS = 12
WCAP = 128
COLS = 256
HALF = 128
VMEM_BYTES = 56 * 1024 * 1024

epsilon = 1e-06
big_negative = -1e30

AXES = ("gx", "gy", "gz")
MESH = pl.DeviceIdType.MESH
f32 = jnp.float32
bf16 = jnp.bfloat16


def nn(a, b):
    return lax.dot_general(a, b, (((1,), (0,)), ((), ())), preferred_element_type=f32)


def nt(a, b):
    return lax.dot_general(a, b, (((1,), (1,)), ((), ())), preferred_element_type=f32)


def tn(a, b):
    return lax.dot_general(a, b, (((0,), (0,)), ((), ())), preferred_element_type=f32)


def direction(k):
    return (k // 4, k // 2 % 2, k % 2)


def neighbours(sizes):
    here = [lax.axis_index(a) for a in AXES]
    found = []
    for k in range(1, 8):
        step = direction(k)
        up = tuple(here[i] + step[i] for i in range(3))
        down = tuple(here[i] - step[i] for i in range(3))
        has_up = functools.reduce(
            jnp.logical_and, [up[i] < sizes[i] for i in range(3) if step[i]]
        )
        has_down = functools.reduce(
            jnp.logical_and, [down[i] >= 0 for i in range(3) if step[i]]
        )
        found.append((up, down, has_up, has_down))
    return found


def greet(found, partners):
    barrier = pltpu.get_barrier_semaphore()
    count = jnp.int32(len(partners))
    for up, down, has_up, has_down in found:
        @pl.when(has_up)
        def _():
            pl.semaphore_signal(barrier, inc=1, device_id=up, device_id_type=MESH)

        @pl.when(has_down)
        def _():
            pl.semaphore_signal(barrier, inc=1, device_id=down, device_id_type=MESH)

        count = count + has_up.astype(jnp.int32) + has_down.astype(jnp.int32)
    for partner in partners:
        pl.semaphore_signal(barrier, inc=1, device_id=partner, device_id_type=MESH)
    pl.semaphore_wait(barrier, count)


def block_kernel(sizes, orders, bits, places, *refs):
    parts, pairs = len(orders), len(bits)
    stages = pairs + 1
    deep = sizes[2]
    refs = list(refs)

    def take(n):
        out = refs[:n]
        del refs[:n]
        return out

    tok_ref, gout_ref, send_ref, wrow_ref, gain_ref, wqkv_hbm, wout_hbm = take(7)
    own_ref, back_ref, place_ref, gsum_ref = take(4)
    if parts:
        gqkv_ref, gproj_ref = take(2)
    else:
        (grad_ref,) = take(1)
    buf, table, wqkv_ref, wout_ref, wcol, pick = take(6)
    xs, unit, normed, normed_t, inv, packed, delta, mixed, mixed_t, dpacked, dnormed = take(11)
    bg, ret, held_probs = take(3)
    gheld, gcome, gcome_z = take(3)
    load_sem, send_sem, recv_sem, ret_send, ret_recv, gain_send, gain_recv = take(7)
    gain_send_z, gain_recv_z = take(2)
    if parts:
        piece, part_send, part_recv, send_z, recv_z, come_z = take(6)
        come = take(pairs)
        held = take(stages)

    found = neighbours(sizes)
    count, width = tok_ref.shape
    double = 2 * width
    cap = send_ref.shape[2]
    span = count + 7 * cap
    slots = wrow_ref.shape[1]
    windows = slots // WCAP
    head_dim = width // HEADS
    pair = 2 * head_dim
    scale = head_dim ** (-0.5)
    here = [lax.axis_index(a) for a in AXES]

    def own_bit(bit):
        axis, distance = bit
        return here[axis] // distance % 2

    def partner(bit):
        axis, distance = bit
        return tuple(
            here[i] + distance * (1 - 2 * own_bit(bit)) if i == axis else here[i] for i in range(3)
        )

    def forward_copy(h, k):
        return pltpu.make_async_remote_copy(
            src_ref=buf.at[h, pl.ds(k * cap, cap)],
            dst_ref=table.at[h, pl.ds(k * cap, cap)],
            send_sem=send_sem.at[7 * h + k],
            recv_sem=recv_sem.at[7 * h + k],
            device_id=found[k][0],
            device_id_type=MESH,
        )

    def along_z(d):
        return (here[0], here[1], lax.rem(here[2] + d, deep))

    def return_copy(h, k):
        return pltpu.make_async_remote_copy(
            src_ref=ret.at[h, pl.ds(k * cap, cap)],
            dst_ref=back_ref.at[h, pl.ds(k * cap, cap)],
            send_sem=ret_send.at[7 * h + k],
            recv_sem=ret_recv.at[7 * h + k],
            device_id=found[k][1],
            device_id_type=MESH,
        )

    def part_copy_z(p, d):
        return pltpu.make_async_remote_copy(
            src_ref=held[pairs].at[p, pl.ds(along_z(d)[2], 1)],
            dst_ref=come_z.at[p, pl.ds(d - 1, 1)],
            send_sem=send_z.at[p * (deep - 1) + d - 1],
            recv_sem=recv_z.at[p * (deep - 1) + d - 1],
            device_id=along_z(d),
            device_id_type=MESH,
        )

    def gain_copy_z(d):
        return pltpu.make_async_remote_copy(
            src_ref=gheld.at[pairs],
            dst_ref=gcome_z.at[d - 1],
            send_sem=gain_send_z.at[d - 1],
            recv_sem=gain_recv_z.at[d - 1],
            device_id=along_z(d),
            device_id_type=MESH,
        )

    def part_copy(p, s):
        bit = orders[p][s]
        half = come[s].shape[1]
        return pltpu.make_async_remote_copy(
            src_ref=held[s].at[p, pl.ds((1 - own_bit(bit)) * half, half)],
            dst_ref=come[s].at[p],
            send_sem=part_send.at[p * pairs + s],
            recv_sem=part_recv.at[p * pairs + s],
            device_id=partner(bit),
            device_id_type=MESH,
        )

    def gain_copy(s):
        return pltpu.make_async_remote_copy(
            src_ref=gheld.at[s],
            dst_ref=gcome.at[s],
            send_sem=gain_send.at[s],
            recv_sem=gain_recv.at[s],
            device_id=partner(bits[s]),
            device_id_type=MESH,
        )

    loads = [
        pltpu.make_async_copy(wqkv_hbm, wqkv_ref, load_sem.at[0]),
        pltpu.make_async_copy(wout_hbm, wout_ref, load_sem.at[1]),
    ]
    for load in loads:
        load.start()

    send_row = jnp.concatenate([send_ref[k] for k in range(7)], axis=1)
    place = (
        lax.broadcasted_iota(jnp.int32, (count, 7 * cap), 0) == send_row
    ).astype(f32).astype(bf16)
    place_ref[...] = place
    buf[0] = tn(place, tok_ref[...]).astype(bf16)
    greet(found, [partner(bit) for bit in bits] + [along_z(d) for d in range(1, deep)])

    def start_forward(h):
        for k in (6, 5, 4, 3, 2, 1, 0):
            @pl.when(found[k][2])
            def _():
                forward_copy(h, k).start()

    def wait_forward(h):
        for k in range(7):
            @pl.when(found[k][3])
            def _():
                forward_copy(h, k).wait_recv()

    start_forward(0)
    buf[1] = tn(place, gout_ref[...]).astype(bf16)
    start_forward(1)
    for k in range(7):
        @pl.when(jnp.logical_not(found[k][3]))
        def _():
            for h in range(2):
                table[h, pl.ds(k * cap, cap), :] = jnp.zeros((cap, width), bf16)

        @pl.when(jnp.logical_not(found[k][2]))
        def _():
            for h in range(2):
                back_ref[h, pl.ds(k * cap, cap), :] = jnp.zeros((cap, width), bf16)
    wcol[...] = jnp.broadcast_to(wrow_ref[...], (8, slots)).T[:, :1]
    pick[...] = (
        lax.broadcasted_iota(jnp.int32, (slots, span), 1) == wcol[...]
    ).astype(f32).astype(bf16)
    gain_row = gain_ref[...].reshape(1, width)
    for h, own in enumerate((tok_ref, gout_ref)):
        @pl.loop(0, width // COLS, unroll=True)
        def _(j):
            cols = pl.ds(pl.multiple_of(j * COLS, COLS), COLS)
            into = pl.ds(pl.multiple_of(h * width + j * COLS, COLS), COLS)
            xs[:, into] = nn(pick[:, :count], own[:, cols]).astype(bf16)
    for load in loads:
        load.wait()

    def fill(h):
        @pl.loop(0, width // COLS, unroll=True)
        def _(j):
            cols = pl.ds(pl.multiple_of(j * COLS, COLS), COLS)
            into = pl.ds(pl.multiple_of(h * width + j * COLS, COLS), COLS)
            come_in = nn(pick[:, count:], table[h, :, cols])
            xs[:, into] = (xs[:, into].astype(f32) + come_in).astype(bf16)

    wait_forward(0)
    fill(0)

    @pl.loop(0, windows, unroll=2)
    def _(w):
        rows = pl.ds(pl.multiple_of(w * WCAP, WCAP), WCAP)
        floats = xs[rows, :width].astype(f32)
        centred = floats - jnp.mean(floats, axis=-1, keepdims=True)
        inv_std = lax.rsqrt(jnp.mean(centred * centred, axis=-1, keepdims=True) + epsilon)
        u = centred * inv_std
        unit[rows, :] = u
        inv[rows, :] = inv_std
        normed[rows, :] = (u * gain_row).astype(bf16)

    normed_t[...] = normed[...].T

    @pl.loop(0, 3 * width // COLS, unroll=3)
    def _(j):
        cols = pl.ds(pl.multiple_of(j * COLS, COLS), COLS)
        packed[:, cols] = nn(normed[...], wqkv_ref[:, cols]).astype(bf16)

    first = lax.broadcasted_iota(jnp.int32, (WCAP, pair), 1) < head_dim
    none = jnp.zeros((WCAP, pair), bf16)

    def split(t):
        return jnp.concatenate([jnp.where(first, t, none), jnp.where(first, none, t)], axis=0)

    def join(t):
        return jnp.where(first, t[:WCAP], t[WCAP:])

    def both_heads(w):
        return pl.ds(pl.multiple_of(w * 2 * WCAP, 2 * WCAP), 2 * WCAP)

    def forward(w, j, valid):
        rows = pl.ds(pl.multiple_of(w * WCAP, WCAP), WCAP)
        at = j * pair
        q = packed[rows, at:at + pair]
        k2 = split(packed[rows, width + at:width + at + pair])
        v2 = split(packed[rows, 2 * width + at:2 * width + at + pair])
        scores = nt(k2, q).reshape(2, WCAP, WCAP) * scale
        scores = jnp.where(valid, scores, big_negative)
        top = jnp.max(scores, axis=1, keepdims=True)
        expo = jnp.exp(scores - top)
        probs = expo * (1.0 / jnp.sum(expo, axis=1, keepdims=True))
        probs = probs.reshape(2 * WCAP, WCAP)
        held_probs[j, both_heads(w), :] = probs
        mixed[rows, at:at + pair] = tn(probs.astype(bf16), v2).astype(bf16)

    def backward(w, j):
        rows = pl.ds(pl.multiple_of(w * WCAP, WCAP), WCAP)
        at = j * pair
        q = packed[rows, at:at + pair]
        k2 = split(packed[rows, width + at:width + at + pair])
        v2 = split(packed[rows, 2 * width + at:2 * width + at + pair])
        g = delta[rows, at:at + pair]
        probs = held_probs[j, both_heads(w), :]
        weights = probs.astype(bf16)
        probs = probs.reshape(2, WCAP, WCAP)
        dweights = nt(v2, g).reshape(2, WCAP, WCAP)
        total = jnp.sum(dweights * probs, axis=1, keepdims=True)
        dscaled = (probs * (dweights - total) * scale).reshape(2 * WCAP, WCAP).astype(bf16)
        dpacked[rows, at:at + pair] = tn(dscaled, k2).astype(bf16)
        dpacked[rows, width + at:width + at + pair] = join(nn(dscaled, q)).astype(bf16)
        dpacked[rows, 2 * width + at:2 * width + at + pair] = join(nn(weights, g)).astype(bf16)

    def backward_group(group):
        @pl.loop(0, windows // 2)
        def _(i):
            for w in (2 * i, 2 * i + 1):
                for j in (2 * group, 2 * group + 1):
                    backward(w, j)

    @pl.loop(0, windows)
    def _(w):
        valid = (wcol[pl.ds(pl.multiple_of(w * WCAP, WCAP), WCAP), :] >= 0)[None]
        for j in range(HEADS // 2):
            forward(w, j, valid)

    @pl.loop(0, width // COLS, unroll=True)
    def _(j):
        cols = pl.ds(pl.multiple_of(j * COLS, COLS), COLS)
        out = nn(mixed[...], wout_ref[:, cols])
        bg[:, cols] = (xs[:, cols].astype(f32) + out).astype(bf16)

    received = (
        lax.broadcasted_iota(jnp.int32, (7 * cap, slots), 0) + count == wrow_ref[...]
    ).astype(f32).astype(bf16)

    def collect_returns(h):
        for j in range(width // COLS):
            cols = slice(j * COLS, (j + 1) * COLS)
            into = slice(h * width + j * COLS, h * width + (j + 1) * COLS)
            ret[h, :, cols] = nn(received, bg[:, into]).astype(bf16)

    def start_returns(h, members):
        for k in members:
            @pl.when(found[k][3])
            def _():
                return_copy(h, k).start()

    collect_returns(0)
    start_returns(0, (6, 5, 4, 3, 2, 1, 0))

    wait_forward(1)
    fill(1)

    @pl.loop(0, width // COLS, unroll=True)
    def _(j):
        cols = pl.ds(pl.multiple_of(j * COLS, COLS), COLS)
        delta[:, cols] = nt(xs[:, width:], wout_ref[cols, :]).astype(bf16)

    def first_column(p):
        if p < 3:
            return 3 * width + p * COLS
        return (p % 3) * width + (p // 3 - 1) * COLS

    def gradient(at):
        if at < 3 * width:
            return nn(normed_t[...], dpacked[:, at:at + COLS])
        return nn(mixed_t[...], xs[:, at - 2 * width:at - 2 * width + COLS])

    def open_parts(members):
        for p in members:
            piece[p % 2] = gradient(first_column(p))
            rows = held[0].shape[2] // 2
            for c, position in enumerate(places[p]):
                both = piece[p % 2, c * rows:(c + 1) * rows, :]
                held[0][p, position] = jnp.concatenate(
                    [both[:, :HALF], both[:, HALF:]], axis=0
                ).astype(bf16)
            part_copy(p, 0).start()

    def advance(members, s):
        for p in members:
            if s < pairs:
                part_copy(p, s).wait_recv()
                half = come[s].shape[1]
                base = own_bit(orders[p][s]) * half
                step = min(half, 4)

                @pl.loop(0, half // step)
                def _(i):
                    mine = held[s][p, pl.ds(base + i * step, step)].astype(f32)
                    theirs = come[s][p, pl.ds(i * step, step)].astype(f32)
                    held[s + 1][p, pl.ds(i * step, step)] = (mine + theirs).astype(bf16)

                if s + 1 < pairs:
                    part_copy(p, s + 1).start()
                else:
                    for d in range(1, deep):
                        part_copy_z(p, d).start()
            else:
                total = held[s][p, pl.ds(here[2], 1)].astype(f32)[0]
                for d in range(1, deep):
                    part_copy_z(p, d).wait_recv()
                    total = total + come_z[p, d - 1].astype(f32)
                rows = total.shape[0] // 2
                for i in range(2):
                    at = first_column(p) + i * HALF
                    value = total[i * rows:(i + 1) * rows]
                    if at < 3 * width:
                        gqkv_ref[:, at:at + HALF] = value
                    else:
                        gproj_ref[:, at - 3 * width:at - 3 * width + HALF] = value

    def advance_gain(s):
        if s < pairs:
            gain_copy(s).wait_recv()
            gheld[s + 1] = gheld[s] + gcome[s]
            if s + 1 < pairs:
                gain_copy(s + 1).start()
            else:
                for d in range(1, deep):
                    gain_copy_z(d).start()
        else:
            total = gheld[s]
            for d in range(1, deep):
                gain_copy_z(d).wait_recv()
                total = total + gcome_z[d - 1]
            gsum_ref[...] = total

    groups = HEADS // 4
    waves = [range(3 * i, 3 * i + 3) for i in range(parts // 3)]
    stage_of = {}

    def open_wave(i):
        if parts:
            open_parts(waves[i])
            turn()
            stage_of[i] = 0

    def turn():
        for i in sorted(stage_of):
            if stage_of[i] < stages:
                advance(waves[i], stage_of[i])
                stage_of[i] += 1

    mixed_t[...] = mixed[...].T
    open_wave(0)
    for group in range(groups):
        backward_group(group)
        open_wave(group + 1)

    @pl.loop(0, width // COLS, unroll=True)
    def _(j):
        cols = pl.ds(pl.multiple_of(j * COLS, COLS), COLS)
        dnormed[:, cols] = nt(dpacked[...], wqkv_ref[cols, :]).astype(bf16)

    turn()
    gheld[0] = jnp.zeros((8, width), f32)

    @pl.loop(0, windows, unroll=2)
    def _(w):
        rows = pl.ds(pl.multiple_of(w * WCAP, WCAP), WCAP)
        dn = dnormed[rows, :].astype(f32)
        u = unit[rows, :]
        gheld[0] += jnp.sum((dn * u).reshape(WCAP // 8, 8, width), axis=0)
        dunit = dn * gain_row
        dcentre = inv[rows, :] * (
            dunit
            - jnp.mean(dunit, axis=-1, keepdims=True)
            - u * jnp.mean(dunit * u, axis=-1, keepdims=True)
        )
        bg[rows, width:] = (xs[rows, width:].astype(f32) + dcentre).astype(bf16)

    gain_copy(0).start()
    turn()
    collect_returns(1)
    start_returns(1, (6, 5, 4, 3, 2, 1, 0))
    advance_gain(0)
    turn()
    kept = (
        lax.broadcasted_iota(jnp.int32, (count, slots), 0) == wrow_ref[...]
    ).astype(f32).astype(bf16)
    for j in range(double // COLS):
        cols = slice(j * COLS, (j + 1) * COLS)
        own_ref[:, cols] = nn(kept, bg[:, cols]).astype(bf16)
    if not parts:
        for j in range(4 * width // COLS):
            grad_ref[:, j * COLS:(j + 1) * COLS] = gradient(j * COLS)
    for s in range(1, stages):
        advance_gain(s)
        turn()

    for h in range(2):
        for k in range(7):
            @pl.when(found[k][2])
            def _():
                return_copy(h, k).wait_recv()
                forward_copy(h, k).wait_send()

            @pl.when(found[k][3])
            def _():
                return_copy(h, k).wait_send()
    for s in range(pairs):
        for p in range(parts):
            part_copy(p, s).wait_send()
        gain_copy(s).wait_send()
    for d in range(1, deep):
        for p in range(parts):
            part_copy_z(p, d).wait_send()
        gain_copy_z(d).wait_send()


def finish_kernel(sizes, own_ref, back_ref, place_ref, gsum_ref, *refs):
    many = len(refs) // 2 - 1
    given, (block_ref, gtok_ref, gain_ref, *final) = refs[:many], refs[many:]
    width = block_ref.shape[1]
    chunk = gain_ref.shape[1]
    place = place_ref[...]
    block_ref[...] = (
        own_ref[:, :width].astype(f32) + nn(place, back_ref[0])
    ).astype(bf16)
    gtok_ref[...] = (
        own_ref[:, width:].astype(f32) + nn(place, back_ref[1])
    ).astype(bf16)
    me = (lax.axis_index("gx") * sizes[1] + lax.axis_index("gy")) * sizes[2] + lax.axis_index("gz")
    rolled = pltpu.roll(gsum_ref[...], lax.rem(width - me * chunk, width), 1)
    gain_ref[...] = jnp.sum(rolled, axis=0, keepdims=True)[:, :chunk]
    for source, target in zip(given, final):
        target[...] = source[...]


def on_device(sizes, tokens, norm_gain, w_qkv, w_out, send_rows, window_rows, grad_out):
    count, width = tokens.shape
    slots = window_rows.shape[1]
    cap = send_rows.shape[2]
    span = count + 7 * cap
    devices = sizes[0] * sizes[1] * sizes[2]
    vmem = pl.BlockSpec(memory_space=pltpu.VMEM)
    params = functools.partial(pltpu.CompilerParams, vmem_limit_bytes=VMEM_BYTES)

    by_axis = [[(a, 1 << i) for i in range(sizes[a].bit_length() - 1)] for a in range(3)]
    x_bits, y_bits, z_bits = by_axis
    bits = y_bits + x_bits
    chunk = width // devices
    grouped = (
        all(1 << len(b) == n for b, n in zip(by_axis, sizes))
        and len(y_bits) > 0
        and sizes[2] > 1
        and chunk * devices == width
        and chunk % 8 == 0
    )
    parts = 4 * width // COLS
    orders, places = [], None
    if grouped:
        rest = y_bits[1:]
        kinds = [y_bits[:1] + x_bits + rest, y_bits[:1] + rest + x_bits]
        orders = [kinds[p % 2] for p in range(parts)]

        def position(order, c):
            at = (c // (sizes[1] * sizes[2]), c // sizes[2] % sizes[1], c % sizes[2])
            value = 0
            for axis, distance in order:
                value = 2 * value + at[axis] // distance % 2
            return value * sizes[2] + at[2]

        places = [[position(order, c) for c in range(devices)] for order in orders]

    pairs, deep = len(bits), sizes[2]
    anywhere = pl.BlockSpec(memory_space=pl.ANY)
    out_shape = [
        jax.ShapeDtypeStruct((count, 2 * width), bf16),
        jax.ShapeDtypeStruct((2, 7 * cap, width), bf16),
        jax.ShapeDtypeStruct((count, 7 * cap), bf16),
        jax.ShapeDtypeStruct((8, width), f32),
    ]
    if grouped:
        sums = [
            jax.ShapeDtypeStruct((chunk, 3 * width), f32),
            jax.ShapeDtypeStruct((chunk, width), f32),
        ]
    else:
        sums = [jax.ShapeDtypeStruct((width, 4 * width), f32)]
    scratch = [
        pltpu.VMEM((2, 7 * cap, width), bf16),
        pltpu.VMEM((2, 7 * cap, width), bf16),
        pltpu.VMEM((width, 3 * width), bf16),
        pltpu.VMEM((width, width), bf16),
        pltpu.VMEM((slots, 1), jnp.int32),
        pltpu.VMEM((slots, span), bf16),
        pltpu.VMEM((slots, 2 * width), bf16),
        pltpu.VMEM((slots, width), f32),
        pltpu.VMEM((slots, width), bf16),
        pltpu.VMEM((width, slots), bf16),
        pltpu.VMEM((slots, 1), f32),
        pltpu.VMEM((slots, 3 * width), bf16),
        pltpu.VMEM((slots, width), bf16),
        pltpu.VMEM((slots, width), bf16),
        pltpu.VMEM((width, slots), bf16),
        pltpu.VMEM((slots, 3 * width), bf16),
        pltpu.VMEM((slots, width), bf16),
        pltpu.VMEM((slots, 2 * width), bf16),
        pltpu.VMEM((2, 7 * cap, width), bf16),
        pltpu.VMEM((HEADS // 2, 2 * slots, WCAP), f32),
        pltpu.VMEM((pairs + 1, 8, width), f32),
        pltpu.VMEM((pairs, 8, width), f32),
        pltpu.VMEM((deep - 1, 8, width), f32),
        pltpu.SemaphoreType.DMA((2,)),
        pltpu.SemaphoreType.DMA((14,)),
        pltpu.SemaphoreType.DMA((14,)),
        pltpu.SemaphoreType.DMA((14,)),
        pltpu.SemaphoreType.DMA((14,)),
        pltpu.SemaphoreType.DMA((pairs,)),
        pltpu.SemaphoreType.DMA((pairs,)),
        pltpu.SemaphoreType.DMA((deep - 1,)),
        pltpu.SemaphoreType.DMA((deep - 1,)),
    ]
    if grouped:
        slab = (2 * chunk, HALF)
        scratch += [pltpu.VMEM((2, width, COLS), f32)]
        scratch += [pltpu.SemaphoreType.DMA((parts * pairs,))] * 2
        scratch += [pltpu.SemaphoreType.DMA((parts * (deep - 1),))] * 2
        scratch += [pltpu.VMEM((parts, deep - 1) + slab, bf16)]
        scratch += [pltpu.VMEM((parts, devices >> (s + 1)) + slab, bf16) for s in range(pairs)]
        scratch += [pltpu.VMEM((parts, devices >> s) + slab, bf16) for s in range(pairs + 1)]
    own, back, place, gain_sum, *grads = pl.pallas_call(
        functools.partial(block_kernel, sizes, orders, bits, places),
        out_shape=tuple(out_shape + sums),
        in_specs=[vmem] * 5 + [anywhere] * 2,
        out_specs=(vmem,) * len(out_shape + sums),
        scratch_shapes=scratch,
        compiler_params=params(collective_id=0, has_side_effects=True),
        name="block",
    )(tokens, grad_out, jnp.transpose(send_rows, (1, 0, 2)), window_rows, norm_gain, w_qkv, w_out)

    passed = grads if grouped else []
    final_shape = [jax.ShapeDtypeStruct((count, width), bf16)] * 2
    final_shape += [jax.ShapeDtypeStruct((1, chunk), f32)] + (sums if grouped else [])
    block_out, grad_tokens, grad_gain, *final = pl.pallas_call(
        functools.partial(finish_kernel, sizes),
        out_shape=tuple(final_shape),
        in_specs=[vmem] * (4 + len(passed)),
        out_specs=(vmem,) * len(final_shape),
        compiler_params=params(),
        name="finish",
    )(own, back, place, gain_sum, *passed)
    if grouped:
        grad_qkv, grad_proj = final
    else:
        summed = lax.psum_scatter(grads[0], AXES, scatter_dimension=0, tiled=True)
        grad_qkv, grad_proj = summed[:, :3 * width], summed[:, 3 * width:]
    return (block_out, grad_tokens, grad_gain.reshape(chunk), grad_qkv, grad_proj)


def solution(mesh):
    sizes = tuple(mesh.shape[a] for a in AXES)
    in_specs = (
        P(AXES, None),
        P(),
        P(),
        P(),
        P(AXES, None, None),
        P(AXES, None),
        P(AXES, None),
    )
    out_specs = (
        P(AXES, None),
        P(AXES, None),
        P(AXES),
        P(AXES, None),
        P(AXES, None),
    )
    return jax.shard_map(
        functools.partial(on_device, sizes),
        mesh=mesh,
        in_specs=in_specs,
        out_specs=out_specs,
        check_vma=False,
    )
```
